768 devices in a mesh: gx: 12 (over z), gy: 64 (over y, x, core).
Axes of the slice: x: 4, y: 8, z: 12, core: 2. Of those that a mesh axis runs over, the one named last changes fastest.
Arguments:
- coarse_state: float32 [384, 5, 384, 128], P('gy', None, 'gx')
- fine_state: float32 [12, 2048, 5, 8, 128], P('gx', 'gy')
- fine_count: int32 [12, 64], P('gx'), may hold values from 10 to 32, as said below
- parent_owner: int32 [12, 2048], P('gx'), may hold values from 0 to 63, as said below
- parent_site: int32 [12, 2048], P('gx'), may hold values from 0 to 47, as said below
- fine_half: int32 [12, 2048], P('gx'), may hold values from 0 to 1
Outputs:
- coarse_out: float32 [384, 5, 384, 128], P('gy', None, 'gx')
- fine_out: float32 [12, 2048, 5, 8, 128], P('gx', 'gy')
The draws below stay inside these ranges and needn't reach their ends.
Inputs may be any that keep to these rules, and one draw needn't show every extreme that they name: `fine_count`: slots at or above a device's count are empty. In every gx row one device holds 32 live patches and another 32 // 3. `parent_owner`: A parent lies in the same gx row as its fine patch. The live patches of one device name one owner at most 2 times, and some device names one owner exactly 2 times. `parent_site`: site = (t * 2 + e) * 4 + q: tile t of the owner's 6 tiles, patch column 2 e of its block, quadrant q = 2 qy + qz. Fine patches whose parents one device owns name distinct sites, so fine regions never touch one another or one another's outer neighbour cells.
All inputs are finite; a program needn't handle non-finite values.
Results may differ from the reference program's by a relative error of at most 0.0003.
Values sent between devices are 32-bit elements; how exact they have to be, the bound alone decides.
No kernel may reach another device: no remote copies, remote signals or barrier semaphores. Data moves between devices by JAX's collectives and lax.ppermute only.
A program may use at most 128 MiB of HBM per device.

```python
import jax
import jax.numpy as jnp
from jax import lax

NF = 5
B = 8
SY = 8
SZ = 16
TT = 6
CX = 32
KF = 32
NT = 384
NXC = 384
N_GX = 12
N_GY = 64


def routing_tables(key):
    owner_key, site_key, count_key, low_key, high_key = jax.random.split(key, 5)
    owner_perm = jax.vmap(lambda subkey: jax.random.permutation(subkey, N_GY))(jax.random.split(owner_key, N_GX))
    slot_index = jnp.arange(KF, dtype=jnp.int32)
    shifts = jnp.where(slot_index == 0, 0, (slot_index - 1) % N_GY)
    receivers = jnp.arange(N_GY, dtype=jnp.int32)
    targets = (receivers[:, None] + shifts[None, :]) % N_GY
    owners = owner_perm[:, targets].astype(jnp.int32)
    site_total = TT * (CX // (2 * B)) * 4
    site_perm = jax.vmap(lambda subkey: jax.random.permutation(subkey, site_total))(jax.random.split(site_key, N_GX * N_GY))
    site_perm = site_perm.reshape(N_GX, N_GY * site_total).astype(jnp.int32)
    site_index = owners * site_total + slot_index[None, None, :]
    site_ids = jnp.take_along_axis(site_perm, site_index.reshape(N_GX, N_GY * KF), axis=1)
    counts = jax.random.randint(count_key, (N_GX, N_GY), KF - KF // 6, KF + 1)
    low_pick = jax.random.randint(low_key, (N_GX, 1), 0, N_GY)
    high_pick = (low_pick + jax.random.randint(high_key, (N_GX, 1), 1, N_GY)) % N_GY
    counts = jnp.where(receivers[None, :] == low_pick, KF // 3, counts)
    counts = jnp.where(receivers[None, :] == high_pick, KF, counts)
    return (counts.astype(jnp.int32), owners.reshape(N_GX, N_GY * KF), site_ids.astype(jnp.int32))


def state_fields(key, extent, field_axis, exponent):
    uniform_part = jax.random.uniform(key, extent, jnp.float32, -1.0, 1.0)
    uniform_part = jnp.sign(uniform_part) * jnp.abs(uniform_part) ** exponent
    centre = jnp.array([1.0, 0.0, 0.0, 0.0, 3.0], jnp.float32)
    spread = jnp.array([0.3, 0.4, 0.4, 0.4, 0.5], jnp.float32)
    layout = [1] * len(extent)
    layout[field_axis] = NF
    return centre.reshape(layout) + spread.reshape(layout) * uniform_part


def draw_fine_count(key, part):
    return routing_tables(key)[0]


def draw_parent_owner(key, part):
    return routing_tables(key)[1]


def draw_parent_site(key, part):
    return routing_tables(key)[2]


def draw_coarse_state(key, part):
    key = jax.random.fold_in(key, 11)
    exponent = 1.0
    return state_fields(key, (NT, NF, NXC, SY * SZ), 1, exponent)


def draw_fine_state(key, part):
    key = jax.random.fold_in(key, 23)
    exponent = 1.0
    return state_fields(key, (N_GX, N_GY * KF, NF, B, SY * SZ), 2, exponent)


def set_ends(result, rng, smallest, top_value):
    spot = [jax.random.randint(jax.random.fold_in(rng, axis), (), 0, length) for axis, length in enumerate(result.shape)]
    longest = result.shape.index(max(result.shape))
    next_to = spot[:longest] + [(spot[longest] + 1) % result.shape[longest]] + spot[longest + 1:]
    return result.at[tuple(spot)].set(smallest).at[tuple(next_to)].set(top_value)


def setup_inputs(seed: int = 0) -> dict:
    key_list = jax.random.split(jax.random.key(seed), 7)
    coarse_state = draw_coarse_state(jax.random.fold_in(key_list[6], 71), 0)
    fine_state = draw_fine_state(jax.random.fold_in(key_list[6], 71), 0)
    fine_count = draw_fine_count(jax.random.fold_in(key_list[6], 71), 0)
    parent_owner = draw_parent_owner(jax.random.fold_in(key_list[6], 71), 0)
    parent_site = draw_parent_site(jax.random.fold_in(key_list[6], 71), 0)
    fine_half = set_ends(jax.random.randint(key_list[5], (N_GX, N_GY * KF), 0, 2), jax.random.fold_in(key_list[5], 1), 0, 1).astype(jnp.int32)
    return dict(coarse_state=coarse_state, fine_state=fine_state, fine_count=fine_count, parent_owner=parent_owner, parent_site=parent_site, fine_half=fine_half)


GAMMA = 1.4
STEP_RATIO = 0.1

def euler_flux(states):
    density = states[..., 0, :, :]
    mom_x = states[..., 1, :, :]
    mom_y = states[..., 2, :, :]
    mom_z = states[..., 3, :, :]
    energy = states[..., 4, :, :]
    velocity = mom_x / density
    kinetic = 0.5 * (mom_x * mom_x + mom_y * mom_y + mom_z * mom_z) / density
    pressure = (GAMMA - 1.0) * (energy - kinetic)
    fluxes = jnp.stack([mom_x, mom_x * velocity + pressure, mom_y * velocity, mom_z * velocity, (energy + pressure) * velocity], axis=-3)
    signal = jnp.abs(velocity) + jnp.sqrt(GAMMA * pressure / density)
    return (fluxes, signal)

def limit_edges(center, left_edge, right_edge):
    edge_jump = right_edge - left_edge
    curvature = 6.0 * (center - 0.5 * (left_edge + right_edge))
    extremum = (right_edge - center) * (center - left_edge) <= 0.0
    new_left = jnp.where(edge_jump * curvature > edge_jump * edge_jump, 3.0 * center - 2.0 * right_edge, left_edge)
    new_right = jnp.where(-edge_jump * edge_jump > edge_jump * curvature, 3.0 * center - 2.0 * left_edge, right_edge)
    return (jnp.where(extremum, center, new_left), jnp.where(extremum, center, new_right))

def face_flux(padded):
    length = padded.shape[-2]
    interior = length - 6
    outer_left = padded[..., 0:length - 3, :]
    near_left = padded[..., 1:length - 2, :]
    near_right = padded[..., 2:length - 1, :]
    outer_right = padded[..., 3:length, :]
    edge_values = 7.0 / 12.0 * (near_left + near_right) - 1.0 / 12.0 * (outer_left + outer_right)
    edge_values = jnp.minimum(jnp.maximum(edge_values, jnp.minimum(near_left, near_right)), jnp.maximum(near_left, near_right))
    left_lim, right_lim = limit_edges(padded[..., 2:interior + 4, :], edge_values[..., 0:interior + 2, :], edge_values[..., 1:interior + 3, :])
    state_left = right_lim[..., 0:interior + 1, :]
    state_right = left_lim[..., 1:interior + 2, :]
    flux_left, signal_left = euler_flux(state_left)
    flux_right, signal_right = euler_flux(state_right)
    signal = jnp.maximum(signal_left, signal_right)[..., None, :, :]
    return 0.5 * (flux_left + flux_right) - 0.5 * signal * (state_right - state_left)

def sweep_cells(padded):
    fluxes = face_flux(padded)
    return (padded[..., 3:-3, :] - STEP_RATIO * (fluxes[..., 1:, :] - fluxes[..., :-1, :]), fluxes)

def expand_cross(values):
    leading = values.shape[:-1]
    grid = values.reshape(leading + (SY // 2, 1, SZ // 2, 1))
    grid = jnp.broadcast_to(grid, leading + (SY // 2, 2, SZ // 2, 2))
    return grid.reshape(leading + (SY * SZ,))

def fold_cross(values):
    leading = values.shape[:-1]
    summed = values.reshape(leading + (SY // 2, 2, SZ // 2, 2)).sum(axis=(-3, -1))
    return summed.reshape(leading + (SY // 2 * (SZ // 2),))

def ghost_cells(ghosts):
    cells = expand_cross(ghosts)
    left_side = jnp.stack([cells[:, :, 0], cells[:, :, 1], cells[:, :, 1]], axis=2)
    right_side = jnp.stack([cells[:, :, 2], cells[:, :, 2], cells[:, :, 3]], axis=2)
    return (left_side, right_side)

def fine_steps(fine, ghost_old, ghost_new):
    cells_x = fine.shape[2]
    left_side, right_side = ghost_cells(ghost_old)
    middle, flux_one = sweep_cells(jnp.concatenate([left_side, fine, right_side], axis=2))
    left_side, right_side = ghost_cells(0.5 * (ghost_old + ghost_new))
    final, flux_two = sweep_cells(jnp.concatenate([left_side, middle, right_side], axis=2))
    bound_one = fold_cross(jnp.stack([flux_one[:, :, 0], flux_one[:, :, cells_x]], axis=2))
    bound_two = fold_cross(jnp.stack([flux_two[:, :, 0], flux_two[:, :, cells_x]], axis=2))
    leading = final.shape[:2]
    restricted = final.reshape(leading + (cells_x // 2, 2, SY * SZ)).sum(axis=3)
    restricted = 0.125 * fold_cross(restricted)
    return (final, bound_one, bound_two, restricted)

def reference(coarse_state, fine_state, fine_count, parent_owner, parent_site, fine_half):
    half_cells = B // 2
    quarter = SY // 2 * (SZ // 2)
    pairs = CX // (2 * B)

    def coarse_tile(tile_cells):
        padded = jnp.concatenate([tile_cells[:, -3:], tile_cells, tile_cells[:, :3]], axis=1)
        return sweep_cells(padded)
    coarse_swept, coarse_flux = lax.map(coarse_tile, coarse_state)
    patches = N_GX * N_GY * KF
    row_ids = jnp.repeat(jnp.arange(N_GX, dtype=jnp.int32), N_GY * KF)
    slot_ids = jnp.tile(jnp.arange(KF, dtype=jnp.int32), N_GX * N_GY)
    owner_flat = parent_owner.reshape(patches)
    site_flat = parent_site.reshape(patches)
    half_flat = fine_half.reshape(patches)
    active = slot_ids < jnp.repeat(fine_count.reshape(N_GX * N_GY), KF)
    tile_ids = owner_flat * TT + site_flat // (pairs * 4)
    quadrant = site_flat % 4
    start = row_ids * CX + 2 * (site_flat // 4 % pairs) * B + half_flat * half_cells
    y_cells = jnp.arange(SY // 2, dtype=jnp.int32)
    z_cells = jnp.arange(SZ // 2, dtype=jnp.int32)
    section_ids = ((quadrant // 2)[:, None, None] * (SY // 2) + y_cells[None, :, None]) * SZ + (quadrant % 2)[:, None, None] * (SZ // 2) + z_cells[None, None, :]
    section_ids = section_ids.reshape(patches, quarter)
    offsets = jnp.array([-2, -1, half_cells, half_cells + 1], jnp.int32)
    ghost_x = (start[:, None] + offsets[None, :]) % NXC
    ghost_old = coarse_state[tile_ids[:, None, None], :, ghost_x[:, :, None], section_ids[:, None, :]].transpose(0, 3, 1, 2)
    ghost_new = coarse_swept[tile_ids[:, None, None], :, ghost_x[:, :, None], section_ids[:, None, :]].transpose(0, 3, 1, 2)
    blocks = N_GX * N_GY
    fine_blocks = fine_state.reshape(blocks, KF, NF, B, SY * SZ)
    old_blocks = ghost_old.reshape(blocks, KF, NF, 4, quarter)
    new_blocks = ghost_new.reshape(blocks, KF, NF, 4, quarter)

    def fine_block(packed):
        return fine_steps(packed[0], packed[1], packed[2])
    final, bound_one, bound_two, restricted = lax.map(fine_block, (fine_blocks, old_blocks, new_blocks))
    live_blocks = active.reshape(blocks, KF)[:, :, None, None, None]
    fine_out = jnp.where(live_blocks, final, 0.0).reshape(N_GX, N_GY * KF, NF, B, SY * SZ)
    face_avg = (0.125 * (bound_one + bound_two)).reshape(patches, NF, 2, quarter)
    restricted = restricted.reshape(patches, NF, half_cells, quarter)
    coarse_left = coarse_flux[tile_ids[:, None], :, start[:, None], section_ids]
    coarse_right = coarse_flux[tile_ids[:, None], :, (start + half_cells)[:, None], section_ids]
    left_fix = STEP_RATIO * (coarse_left - face_avg[:, :, 0].transpose(0, 2, 1))
    right_fix = STEP_RATIO * (face_avg[:, :, 1].transpose(0, 2, 1) - coarse_right)
    drop_tile = jnp.where(active, tile_ids, NT)
    coarse_out = coarse_swept.at[drop_tile[:, None], :, ((start - 1) % NXC)[:, None], section_ids].add(left_fix, mode='drop')
    coarse_out = coarse_out.at[drop_tile[:, None], :, (start + half_cells)[:, None], section_ids].add(right_fix, mode='drop')
    covered_x = start[:, None] + jnp.arange(half_cells, dtype=jnp.int32)[None, :]
    coarse_out = coarse_out.at[drop_tile[:, None, None], :, covered_x[:, :, None], section_ids[:, None, :]].set(restricted.transpose(0, 2, 3, 1), mode='drop')
    return (coarse_out, fine_out)
```

```python
import functools

import jax
import jax.numpy as jnp
from jax import lax
from jax.experimental import pallas as pl
from jax.experimental.pallas import tpu as pltpu
from jax.sharding import PartitionSpec as P

SY = 8
SZ = 16
LANES = SY * SZ
FIELDS = 5
TILES = 6
CELLS = 32
FINE = 8
GAMMA = 1.4
STEP_RATIO = 0.1
GHOST_ROWS = 2 * FIELDS
BACK_ROWS = 8
STARTS = ((0, 0, 0), (0, 1, 4), (1, 0, 16), (1, 1, 20))
FACES = (0, 4, 8, 16, 20, 24)
VMEM = 48 * 1024 * 1024


def edge_value(outer_left, near_left, near_right, outer_right):
    value = 7.0 / 12.0 * (near_left + near_right) - 1.0 / 12.0 * (outer_left + outer_right)
    low = jnp.minimum(near_left, near_right)
    high = jnp.maximum(near_left, near_right)
    return jnp.minimum(jnp.maximum(value, low), high)


def limit_edges(center, left_edge, right_edge):
    jump = right_edge - left_edge
    product = jump * (6.0 * (center - 0.5 * (left_edge + right_edge)))
    square = jump * jump
    extremum = (right_edge - center) * (center - left_edge) <= 0.0
    new_left = jnp.where(product > square, 3.0 * center - 2.0 * right_edge, left_edge)
    new_right = jnp.where(-square > product, 3.0 * center - 2.0 * left_edge, right_edge)
    return (jnp.where(extremum, center, new_left), jnp.where(extremum, center, new_right))


def euler_flux(state):
    density, mom_x, mom_y, mom_z, energy = state
    inverse = 1.0 / density
    velocity = mom_x * inverse
    kinetic = 0.5 * (mom_x * mom_x + mom_y * mom_y + mom_z * mom_z) * inverse
    pressure = (GAMMA - 1.0) * (energy - kinetic)
    fluxes = (
        mom_x,
        mom_x * velocity + pressure,
        mom_y * velocity,
        mom_z * velocity,
        (energy + pressure) * velocity,
    )
    signal = jnp.abs(velocity) + jnp.sqrt(GAMMA * pressure * inverse)
    return (fluxes, signal)


def riemann(left, right):
    flux_left, signal_left = euler_flux(left)
    flux_right, signal_right = euler_flux(right)
    half_signal = 0.5 * jnp.maximum(signal_left, signal_right)
    return tuple(
        0.5 * (fl + fr) - half_signal * (r - l)
        for fl, fr, l, r in zip(flux_left, flux_right, left, right)
    )


def lane_index(rows):
    return lax.broadcasted_iota(jnp.int32, (rows, LANES), 1)


def pull_lanes(value, index):
    return jnp.take_along_axis(value, index, axis=1)


def coarse_kernel(
    codes, own, before, after, swept, sending, face_out, cells, fresh, fluxes, table
):
    stride = FIELDS * CELLS
    for f in range(FIELDS):
        for j in range(5):
            cells[j, f] = before[pl.ds(f * 8 + 3 + j, TILES, stride=FIELDS * 8), :]
        for j in range(3):
            cells[37 + j, f] = after[pl.ds(f * 8 + j, TILES, stride=FIELDS * 8), :]

    def load_cells(x, carry):
        for f in range(FIELDS):
            cells[x + 5, f] = own[pl.ds(f * CELLS + x, TILES, stride=stride), :]
        return carry

    lax.fori_loop(0, CELLS, load_cells, 0, unroll=4)

    def limited(j, edge_before):
        edges, lefts, rights = ([], [], [])
        for f in range(FIELDS):
            edge = edge_value(cells[j - 1, f], cells[j, f], cells[j + 1, f], cells[j + 2, f])
            left, right = limit_edges(cells[j, f], edge_before[f], edge)
            edges.append(edge)
            lefts.append(left)
            rights.append(right)
        return (tuple(edges), tuple(lefts), tuple(rights))

    def advance(j, carry):
        edges, rights, flux_before = carry
        edges, lefts, next_rights = limited(j, edges)
        flux = riemann(rights, lefts)
        for f in range(FIELDS):
            fluxes[j - 1, f] = flux[f]
        if flux_before is not None:
            for f in range(FIELDS):
                fresh[j - 1, f] = cells[j - 1, f] - STEP_RATIO * (flux[f] - flux_before[f])
        return (edges, next_rights, flux)

    edges = tuple(
        edge_value(cells[0, f], cells[1, f], cells[2, f], cells[3, f]) for f in range(FIELDS)
    )
    edges, _, rights = limited(2, edges)
    carry = advance(3, (edges, rights, None))
    carry = advance(4, carry)
    carry = advance(5, carry)

    def step(x, carry):
        carry = advance(x + 6, carry)
        for f in range(FIELDS):
            swept[pl.ds(f * CELLS + x, TILES, stride=stride), :] = fresh[x + 5, f]
        return carry

    lax.fori_loop(0, CELLS, step, carry, unroll=4)
    for i, face in enumerate(FACES):
        for f in range(FIELDS):
            face_out[i, f] = fluxes[face + 4, f]

    lane = lane_index(TILES)
    upper_z = (lane & 8) != 0
    upper_y = (lane & 64) != 0

    def swap(low, high, upper, shift):
        return (
            jnp.where(upper, pltpu.roll(high, shift, 1), low),
            jnp.where(upper, high, pltpu.roll(low, LANES - shift, 1)),
        )

    for e, h, start in STARTS:
        for age, source in enumerate((cells, fresh)):
            for f in range(FIELDS):
                c0, c1, c2, c3 = [source[start + 5 + o, f] for o in (-2, -1, 4, 5)]
                c0, c1 = swap(c0, c1, upper_z, 8)
                c2, c3 = swap(c2, c3, upper_z, 8)
                c0, c2 = swap(c0, c2, upper_y, 64)
                c1, c3 = swap(c1, c3, upper_y, 64)
                for q, value in enumerate((c0, c1, c2, c3)):
                    row = (e * 8 + q * 2 + h) * GHOST_ROWS + age * FIELDS + f
                    table[pl.ds(row, TILES, stride=16 * GHOST_ROWS), :] = value

    def send(k, carry):
        for c in range(2):
            code = codes[2 * k + c]

            @pl.when(code >= 0)
            def _():
                base = code * GHOST_ROWS
                sending[k, 3 * c] = table[pl.ds(base, 4), :]
                sending[k, 3 * c + 1] = table[pl.ds(base + 4, 4), :]
                sending[k, 2, 2 * c : 2 * c + 2] = table[pl.ds(base + 8, 2), :]

        return carry

    lax.fori_loop(0, sending.shape[0], send, 0, unroll=2)


def fine_kernel(lookups, count, arrived, fine, fine_out, back, ghosts, cells, packed):
    slots = lookups.shape[0]
    stride = FIELDS * FINE
    live = count[0]

    def fetch(s, carry):
        look = lookups[s]
        owner = lax.shift_right_logical(look, 1)
        pos = look & 1
        ghosts[pl.ds(s, 4, stride=slots), :] = arrived[owner, 3 * pos]
        ghosts[pl.ds(s + 4 * slots, 4, stride=slots), :] = arrived[owner, 3 * pos + 1]
        ghosts[pl.ds(s + 8 * slots, 2, stride=slots), :] = arrived[owner, 2, pl.ds(2 * pos, 2)]
        return carry

    lax.fori_loop(0, slots, fetch, 0, unroll=4)

    lane = lane_index(8)
    fine_y = lax.shift_right_logical(lane, 4)
    fine_z = lane & 15
    spread = lax.shift_right_logical(fine_y, 1) * 16 + lax.shift_right_logical(fine_z, 1)
    even_z = (lane & 1) == 0
    even_y = (lane & 16) == 0
    gather_back = (
        (2 * (fine_y & 3) + lax.shift_right_logical(lane, 6)) * 16
        + 2 * (lane & 7)
        + (lax.shift_right_logical(lane, 3) & 1)
    )

    def pair(first, second, even, shift):
        return jnp.where(even, first, pltpu.roll(second, shift, 1)) + jnp.where(
            even, pltpu.roll(first, LANES - shift, 1), second
        )

    def fold_four(a, b, c, d):
        low = pair(a, b, even_z, 1)
        high = pair(c, d, even_z, 1)
        return pull_lanes(0.125 * pair(low, high, even_y, 16), gather_back)

    def put_ghosts(slot, rows):
        for f in range(FIELDS):
            first, second, third, fourth = [
                pull_lanes(rows[f], spread + (t // 2) * 64 + (t % 2) * 8) for t in range(4)
            ]
            cells[slot, 0, f] = first
            cells[slot, 1, f] = second
            cells[slot, 2, f] = second
            cells[slot, 11, f] = third
            cells[slot, 12, f] = third
            cells[slot, 13, f] = fourth

    def sweep(slot, keep):
        edges = None
        rights = None
        before = None
        bounds = []
        for j in range(1, 12):
            new_edges = [
                edge_value(
                    cells[slot, j - 1, f],
                    cells[slot, j, f],
                    cells[slot, j + 1, f],
                    cells[slot, j + 2, f],
                )
                for f in range(FIELDS)
            ]
            if edges is not None:
                pairs = [
                    limit_edges(cells[slot, j, f], edges[f], new_edges[f]) for f in range(FIELDS)
                ]
                if rights is not None:
                    flux = riemann(rights, [p[0] for p in pairs])
                    if before is None:
                        bounds.append(flux)
                    else:
                        for f in range(FIELDS):
                            keep(
                                j - 4,
                                f,
                                cells[slot, j - 1, f] - STEP_RATIO * (flux[f] - before[f]),
                            )
                    before = flux
                rights = [p[1] for p in pairs]
            edges = new_edges
        bounds.append(before)
        return bounds

    def group(g, carry):
        base = g * (8 * stride)
        old = [ghosts[pl.ds(pl.multiple_of(f * slots + g * 8, 8), 8), :] for f in range(FIELDS)]
        new = [
            ghosts[pl.ds(pl.multiple_of((FIELDS + f) * slots + g * 8, 8), 8), :]
            for f in range(FIELDS)
        ]
        put_ghosts(0, old)
        put_ghosts(1, [0.5 * (o + n) for o, n in zip(old, new)])
        for x in range(FINE):
            for f in range(FIELDS):
                cells[0, x + 3, f] = fine[pl.ds(base + f * FINE + x, 8, stride=stride), :]

        def keep_middle(x, f, value):
            cells[1, x + 3, f] = value

        active = (lax.broadcasted_iota(jnp.int32, (8, LANES), 0) + g * 8) < live
        final = {}

        def keep_final(x, f, value):
            final[x, f] = value
            fine_out[pl.ds(base + f * FINE + x, 8, stride=stride), :] = jnp.where(
                active, value, 0.0
            )

        first = sweep(0, keep_middle)
        second = sweep(1, keep_final)
        rows = []
        for f in range(FIELDS):
            rows.append(fold_four(*[final[2 * t, f] + final[2 * t + 1, f] for t in range(4)]))
        faces = [first[side][f] + second[side][f] for side in range(2) for f in range(FIELDS)]
        faces += [faces[-1], faces[-1]]
        for t in range(3):
            rows.append(fold_four(*faces[4 * t : 4 * t + 4]))
        for r, value in enumerate(rows):
            packed[pl.ds(g * 64 + r, 8, stride=BACK_ROWS), :] = value
        return carry

    lax.fori_loop(0, slots // 8, group, 0)

    def put(s, carry):
        @pl.when(s < live)
        def _():
            target = pl.multiple_of(lookups[s] * BACK_ROWS, BACK_ROWS)
            source = pl.multiple_of(s * BACK_ROWS, BACK_ROWS)
            back[pl.ds(target, BACK_ROWS), :] = packed[pl.ds(source, BACK_ROWS), :]

        return carry

    lax.fori_loop(0, slots, put, 0, unroll=4)


def merge_kernel(codes, came, swept, face_in, out, left_out, field, cover):
    stride = FIELDS * CELLS
    for i in range(TILES * 2):
        cover[8 * i : 8 * i + 8, :] = jnp.zeros((8, LANES), jnp.float32)
    lane = lane_index(8)
    quads = lane & 72

    def scatter(i, carry):
        code = codes[i]

        @pl.when(code >= 0)
        def _():
            quad = lax.shift_right_logical(code, 1) & 3
            offset = lax.shift_right_logical(quad, 1) * 64 + (quad & 1) * 8
            line = lax.shift_right_logical(code, 3) * 8 + (code & 1) * 4
            value = came[pl.ds(pl.multiple_of(i * BACK_ROWS, BACK_ROWS), BACK_ROWS), :]
            inside = quads == offset
            for t in range(4):
                shift = (offset + LANES - ((t // 2) * 64 + (t % 2) * 8)) & (LANES - 1)
                moved = pltpu.roll(value, shift, 1)
                rows = pl.ds(pl.multiple_of((line + t) * 8, 8), 8)
                field[rows, :] = jnp.where(inside, moved, field[rows, :])
            rows = pl.ds(line, 4)
            cover[rows, :] = jnp.where(inside[:4], 1.0, cover[rows, :])

        return carry

    lax.fori_loop(0, codes.shape[0], scatter, 0, unroll=2)

    for t in range(TILES):
        for e in range(2):
            hit = cover[pl.ds(t * 16 + e * 8, 8), :] > 0.5
            for f in range(FIELDS):
                row = t * stride + f * CELLS + e * 16
                value = field[pl.ds((t * 16 + e * 8) * 8 + f, 8, stride=8), :]
                out[row : row + 8, :] = jnp.where(hit, value, swept[row : row + 8, :])
                out[row + 8 : row + 16, :] = swept[row + 8 : row + 16, :]

    for e, h, start in STARTS:
        line = e * 8 + h * 4
        hit = cover[pl.ds(line, TILES, stride=16), :] > 0.5
        for side in range(2):
            for f in range(FIELDS):
                item = side * FIELDS + f
                face = field[
                    pl.ds((line + item % 4) * 8 + FIELDS + item // 4, TILES, stride=128), :
                ]
                coarse = face_in[FACES.index(start + 4 * side), f]
                fix = STEP_RATIO * ((face - coarse) if side else (coarse - face))
                fix = jnp.where(hit, fix, 0.0)
                cell = start + 4 if side else start - 1
                if cell < 0:
                    left_out[f] = fix
                else:
                    rows = pl.ds(f * CELLS + cell, TILES, stride=stride)
                    out[rows, :] = out[rows, :] + fix


def last_kernel(incoming, block, out):
    out[...] = block[...]
    for f in range(FIELDS):
        for t in range(TILES):
            out[t, f, 7:8, :] = block[t, f, 7:8, :] + incoming[f, t : t + 1, :]


def in_vmem():
    return pl.BlockSpec(memory_space=pltpu.VMEM)


def in_smem():
    return pl.BlockSpec(memory_space=pltpu.SMEM)


def shaped(*dims):
    return jax.ShapeDtypeStruct(dims, jnp.float32)


def body(coarse_state, fine_state, fine_count, parent_owner, parent_site, fine_half):
    groups = lax.axis_size("gy")
    rows_x = lax.axis_size("gx")
    me = lax.axis_index("gy")
    slots = fine_state.shape[1]
    params = pltpu.CompilerParams(vmem_limit_bytes=VMEM)

    up = [(i, (i + 1) % rows_x) for i in range(rows_x)]
    down = [(j, i) for i, j in up]
    before = lax.ppermute(coarse_state[:, :, CELLS - 8 :], "gx", up)
    after = lax.ppermute(coarse_state[:, :, :8], "gx", down)

    order = jnp.arange(slots, dtype=jnp.int32)
    joined = parent_owner * LANES + parent_site * 2 + fine_half
    joined = joined.reshape(groups, slots)
    active = order[None, :] < fine_count.reshape(groups, 1)
    hit = (lax.shift_right_logical(joined, 7) == me) & active
    key = order[None, :] * LANES + (joined & (LANES - 1))
    big = slots * LANES
    low = jnp.min(jnp.where(hit, key, big), axis=1)
    high = jnp.max(jnp.where(hit, key, -1), axis=1)
    codes = jnp.stack(
        [
            jnp.where(low < big, low & (LANES - 1), -1),
            jnp.where(high > low, high & (LANES - 1), -1),
        ],
        axis=1,
    ).reshape(2 * groups)
    mine = lax.dynamic_index_in_dim(parent_owner.reshape(groups, slots), me, 0, keepdims=False)
    live = lax.dynamic_slice_in_dim(fine_count.reshape(groups), me, 1, 0)
    twin = (mine[:, None] == mine[None, :]) & (order[None, :] < order[:, None])
    lookups = 2 * mine + jnp.any(twin, axis=1).astype(jnp.int32)

    swept, sending, faces = pl.pallas_call(
        coarse_kernel,
        out_shape=(
            shaped(TILES * FIELDS * CELLS, LANES),
            shaped(groups, 5, 4, LANES),
            shaped(len(FACES), FIELDS, TILES, LANES),
        ),
        in_specs=[in_smem(), in_vmem(), in_vmem(), in_vmem()],
        out_specs=(in_vmem(), in_vmem(), in_vmem()),
        scratch_shapes=[
            pltpu.VMEM((40, FIELDS, TILES, LANES), jnp.float32),
            pltpu.VMEM((40, FIELDS, TILES, LANES), jnp.float32),
            pltpu.VMEM((40, FIELDS, TILES, LANES), jnp.float32),
            pltpu.VMEM((TILES * 16 * GHOST_ROWS, LANES), jnp.float32),
        ],
        compiler_params=params,
        name="coarse",
    )(
        codes,
        coarse_state.reshape(-1, LANES),
        before.reshape(-1, LANES),
        after.reshape(-1, LANES),
    )
    arrived = lax.all_to_all(sending, "gy", split_axis=0, concat_axis=0, tiled=True)

    fine_out, back = pl.pallas_call(
        fine_kernel,
        out_shape=(
            shaped(slots * FIELDS * FINE, LANES),
            shaped(groups * 2 * BACK_ROWS, LANES),
        ),
        in_specs=[in_smem(), in_smem(), in_vmem(), in_vmem()],
        out_specs=(in_vmem(), in_vmem()),
        scratch_shapes=[
            pltpu.VMEM((GHOST_ROWS * slots, LANES), jnp.float32),
            pltpu.VMEM((2, FINE + 6, FIELDS, 8, LANES), jnp.float32),
            pltpu.VMEM((slots * BACK_ROWS, LANES), jnp.float32),
        ],
        compiler_params=params,
        name="fine",
    )(lookups, live, arrived, fine_state.reshape(-1, LANES))
    came = lax.all_to_all(
        back.reshape(groups, 2 * BACK_ROWS, LANES), "gy", split_axis=0, concat_axis=0, tiled=True
    )

    merged, left_fix = pl.pallas_call(
        merge_kernel,
        out_shape=(
            shaped(TILES * FIELDS * CELLS, LANES),
            shaped(FIELDS, TILES, LANES),
        ),
        in_specs=[in_smem(), in_vmem(), in_vmem(), in_vmem()],
        out_specs=(in_vmem(), in_vmem()),
        scratch_shapes=[
            pltpu.VMEM((TILES * 16 * 8, LANES), jnp.float32),
            pltpu.VMEM((TILES * 16, LANES), jnp.float32),
        ],
        compiler_params=params,
        name="merge",
    )(codes, came.reshape(-1, LANES), swept, faces)
    incoming = lax.ppermute(left_fix, "gx", down)
    spec = pl.BlockSpec((TILES, FIELDS, 8, LANES), lambda i: (0, 0, 3, 0))
    coarse_out = pl.pallas_call(
        last_kernel,
        grid=(1,),
        out_shape=shaped(TILES, FIELDS, CELLS, LANES),
        in_specs=[pl.BlockSpec((FIELDS, TILES, LANES), lambda i: (0, 0, 0)), spec],
        out_specs=spec,
        input_output_aliases={1: 0},
        compiler_params=params,
        name="last",
    )(incoming, merged.reshape(TILES, FIELDS, CELLS, LANES))
    return (coarse_out, fine_out.reshape(fine_state.shape))


def solution(mesh):
    placed = (
        P("gy", None, "gx", None),
        P("gx", "gy", None, None, None),
        P("gx", None),
        P("gx", None),
        P("gx", None),
        P("gx", None),
    )
    return jax.shard_map(
        body,
        mesh=mesh,
        in_specs=placed,
        out_specs=(P("gy", None, "gx", None), P("gx", "gy", None, None, None)),
        check_vma=False,
    )
```

```python
import jax
import jax.numpy as jnp
from jax import lax
from jax.experimental import pallas as pl
from jax.experimental.pallas import tpu as pltpu
from jax.sharding import PartitionSpec as P

SY = 8
SZ = 16
LANES = SY * SZ
FIELDS = 5
TILES = 6
CELLS = 32
FINE = 8
GAMMA = 1.4
STEP_RATIO = 0.1
GHOST_ROWS = 2 * FIELDS
BACK_ROWS = 8
STARTS = ((0, 0, 0), (0, 1, 4), (1, 0, 16), (1, 1, 20))
FACES = (0, 4, 8, 16, 20, 24)
ALL_ITEMS = 8
LEFT_ITEMS = 256
VMEM = 48 * 1024 * 1024


def edge_value(outer_left, near_left, near_right, outer_right):
    value = 7.0 / 12.0 * (near_left + near_right) - 1.0 / 12.0 * (outer_left + outer_right)
    low = jnp.minimum(near_left, near_right)
    high = jnp.maximum(near_left, near_right)
    return jnp.minimum(jnp.maximum(value, low), high)


def limit_edges(center, left_edge, right_edge):
    down = center - left_edge
    up = right_edge - center
    twice_down = down + down
    twice_up = up + up
    new_down = jnp.maximum(jnp.minimum(down, twice_up), 0.0) + jnp.minimum(
        jnp.maximum(down, twice_up), 0.0
    )
    new_up = jnp.maximum(jnp.minimum(up, twice_down), 0.0) + jnp.minimum(
        jnp.maximum(up, twice_down), 0.0
    )
    return (center - new_down, center + new_up)


def euler_flux(state):
    density, mom_x, mom_y, mom_z, energy = state
    inverse = 1.0 / density
    velocity = mom_x * inverse
    kinetic = 0.5 * (mom_x * mom_x + mom_y * mom_y + mom_z * mom_z) * inverse
    pressure = (GAMMA - 1.0) * (energy - kinetic)
    fluxes = (
        mom_x,
        mom_x * velocity + pressure,
        mom_y * velocity,
        mom_z * velocity,
        (energy + pressure) * velocity,
    )
    signal = jnp.abs(velocity) + jnp.sqrt(GAMMA * pressure * inverse)
    return (fluxes, signal)


def double_flux(left, right):
    flux_left, signal_left = euler_flux(left)
    flux_right, signal_right = euler_flux(right)
    signal = jnp.maximum(signal_left, signal_right)
    return tuple(
        (fl + fr) - signal * (r - l) for fl, fr, l, r in zip(flux_left, flux_right, left, right)
    )


def lane_index(rows):
    return lax.broadcasted_iota(jnp.int32, (rows, LANES), 1)


def pull_lanes(value, index):
    return jnp.take_along_axis(value, index, axis=1)


def swept_cells(cell, first, last):
    values = {x: cell(x) for x in range(first - 3, last + 4)}
    edges = {}
    for x in range(first - 2, last + 2):
        edges[x] = [
            edge_value(*(values[x + o][f] for o in (-1, 0, 1, 2))) for f in range(FIELDS)
        ]
    limits = {}
    for x in range(first - 1, last + 2):
        limits[x] = [
            limit_edges(values[x][f], edges[x - 1][f], edges[x][f]) for f in range(FIELDS)
        ]
    flux = {}
    for x in range(first, last + 2):
        flux[x] = double_flux([p[1] for p in limits[x - 1]], [p[0] for p in limits[x]])
    return {
        x: [
            values[x][f] - 0.5 * STEP_RATIO * (flux[x + 1][f] - flux[x][f]) for f in range(FIELDS)
        ]
        for x in range(first, last + 1)
    }


def own_cell(own):
    def cell(x):
        return [
            own[pl.ds(f * CELLS + x, TILES, stride=FIELDS * CELLS), :] for f in range(FIELDS)
        ]

    return cell


def write_boxes(table, e, h, old, new):
    lane = lane_index(TILES)
    upper_z = (lane & 8) != 0
    upper_y = (lane & 64) != 0

    def swap(low, high, upper, shift):
        return (
            jnp.where(upper, pltpu.roll(high, shift, 1), low),
            jnp.where(upper, high, pltpu.roll(low, LANES - shift, 1)),
        )

    for age, source in enumerate((old, new)):
        for f in range(FIELDS):
            c0, c1, c2, c3 = [source[o][f] for o in range(4)]
            c0, c1 = swap(c0, c1, upper_z, 8)
            c2, c3 = swap(c2, c3, upper_z, 8)
            c0, c2 = swap(c0, c2, upper_y, 64)
            c1, c3 = swap(c1, c3, upper_y, 64)
            for q, value in enumerate((c0, c1, c2, c3)):
                row = (e * 8 + q * 2 + h) * GHOST_ROWS + age * FIELDS + f
                table[pl.ds(row, TILES, stride=16 * GHOST_ROWS), :] = value


def inner_kernel(own, table, kept):
    cell = own_cell(own)
    new = {}
    for first, last in ((8, 9), (14, 15), (18, 21), (24, 25)):
        new.update(swept_cells(cell, first, last))
    for x in (8, 9):
        for f in range(FIELDS):
            kept[x - 8, f] = new[x][f]
    for e, h, start in STARTS[2:]:
        where = [start + o for o in (-2, -1, 4, 5)]
        write_boxes(table, e, h, [cell(x) for x in where], [new[x] for x in where])


def edge_kernel(codes, own, before, kept, table_in, table, sending):
    inner = own_cell(own)

    def cell(x):
        if x >= 0:
            return inner(x)
        return [before[pl.ds(f * 8 + 8 + x, TILES, stride=FIELDS * 8), :] for f in range(FIELDS)]

    new = swept_cells(cell, -2, 5)
    for x in (8, 9):
        new[x] = [kept[x - 8, f] for f in range(FIELDS)]
    for e, h, start in STARTS[:2]:
        where = [start + o for o in (-2, -1, 4, 5)]
        write_boxes(table, e, h, [cell(x) for x in where], [new[x] for x in where])

    def send(k, carry):
        for c in range(2):
            base = jnp.maximum(codes[2 * k + c], 0) * GHOST_ROWS
            sending[k, 3 * c] = table[pl.ds(base, 4), :]
            sending[k, 3 * c + 1] = table[pl.ds(base + 4, 4), :]
            sending[k, 2, 2 * c : 2 * c + 2] = table[pl.ds(base + 8, 2), :]
        return carry

    lax.fori_loop(0, sending.shape[0], send, 0, unroll=8)


def coarse_kernel(codes, own, before, after, table, swept, face_out, lists, cells, fluxes):
    stride = FIELDS * CELLS
    for f in range(FIELDS):
        for j in range(3):
            cells[j, f] = before[pl.ds(f * 8 + 5 + j, TILES, stride=FIELDS * 8), :]
            cells[35 + j, f] = after[pl.ds(f * 8 + j, TILES, stride=FIELDS * 8), :]

    def load_cells(x, carry):
        for f in range(FIELDS):
            cells[x + 3, f] = own[pl.ds(f * CELLS + x, TILES, stride=stride), :]
        return carry

    lax.fori_loop(0, CELLS, load_cells, 0, unroll=4)

    def limited(j, edge_before):
        edges, lefts, rights = ([], [], [])
        for f in range(FIELDS):
            edge = edge_value(cells[j - 1, f], cells[j, f], cells[j + 1, f], cells[j + 2, f])
            left, right = limit_edges(cells[j, f], edge_before[f], edge)
            edges.append(edge)
            lefts.append(left)
            rights.append(right)
        return (tuple(edges), tuple(lefts), tuple(rights))

    def advance(j, edges, rights):
        edges, lefts, next_rights = limited(j, edges)
        flux = double_flux(rights, lefts)
        for f in range(FIELDS):
            fluxes[j - 3, f] = flux[f]
        return (edges, next_rights, flux)

    edges = tuple(
        edge_value(cells[0, f], cells[1, f], cells[2, f], cells[3, f]) for f in range(FIELDS)
    )
    edges, _, rights = limited(2, edges)
    carry = advance(3, edges, rights)

    def step(x, carry):
        edges, rights, flux_before = carry
        edges, rights, flux = advance(x + 4, edges, rights)
        for f in range(FIELDS):
            swept[pl.ds(f * CELLS + x, TILES, stride=stride), :] = cells[
                x + 3, f
            ] - 0.5 * STEP_RATIO * (flux[f] - flux_before[f])
        return (edges, rights, flux)

    lax.fori_loop(0, CELLS, step, carry, unroll=4)
    for i, face in enumerate(FACES):
        for f in range(FIELDS):
            face_out[i, f] = 0.5 * fluxes[face, f]

    def collect(i, carry):
        total, first = carry
        code = codes[i]
        entry = i * LANES + code
        lists[ALL_ITEMS + total] = entry
        lists[LEFT_ITEMS + first] = entry
        valid = code >= 0
        leftmost = valid & ((code & 9) == 0)
        return (total + valid.astype(jnp.int32), first + leftmost.astype(jnp.int32))

    total, first = lax.fori_loop(0, codes.shape[0], collect, (0, 0), unroll=4)
    lists[0] = total
    lists[1] = first


def fine_kernel(lookups, count, arrived, fine, fine_out, back, ghosts, cells, packed):
    slots = lookups.shape[0]
    stride = FIELDS * FINE
    live = count[0]

    def fetch(s, carry):
        look = lookups[s]
        owner = lax.shift_right_logical(look, 1)
        pos = look & 1
        ghosts[pl.ds(s, 4, stride=slots), :] = arrived[owner, 3 * pos]
        ghosts[pl.ds(s + 4 * slots, 4, stride=slots), :] = arrived[owner, 3 * pos + 1]
        ghosts[pl.ds(s + 8 * slots, 2, stride=slots), :] = arrived[owner, 2, pl.ds(2 * pos, 2)]
        return carry

    lax.fori_loop(0, slots, fetch, 0, unroll=4)

    lane = lane_index(8)
    fine_y = lax.shift_right_logical(lane, 4)
    fine_z = lane & 15
    spread = lax.shift_right_logical(fine_y, 1) * 16 + lax.shift_right_logical(fine_z, 1)
    even_z = (lane & 1) == 0
    even_y = (lane & 16) == 0
    gather_back = (
        (2 * (fine_y & 3) + lax.shift_right_logical(lane, 6)) * 16
        + 2 * (lane & 7)
        + (lax.shift_right_logical(lane, 3) & 1)
    )

    def pair(first, second, even, shift):
        return jnp.where(even, first, pltpu.roll(second, shift, 1)) + jnp.where(
            even, pltpu.roll(first, LANES - shift, 1), second
        )

    def fold_four(scale, a, b, c, d):
        low = pair(a, b, even_z, 1)
        high = pair(c, d, even_z, 1)
        return pull_lanes(scale * pair(low, high, even_y, 16), gather_back)

    def put_ghosts(slot, rows):
        for f in range(FIELDS):
            first, second, third, fourth = [
                pull_lanes(rows[f], spread + (t // 2) * 64 + (t % 2) * 8) for t in range(4)
            ]
            cells[slot, 0, f] = first
            cells[slot, 1, f] = second
            cells[slot, 2, f] = second
            cells[slot, 11, f] = third
            cells[slot, 12, f] = third
            cells[slot, 13, f] = fourth

    def sweep(slot, keep):
        edges = None
        rights = None
        before = None
        bounds = []
        for j in range(1, 12):
            new_edges = [
                edge_value(
                    cells[slot, j - 1, f],
                    cells[slot, j, f],
                    cells[slot, j + 1, f],
                    cells[slot, j + 2, f],
                )
                for f in range(FIELDS)
            ]
            if edges is not None:
                pairs = [
                    limit_edges(cells[slot, j, f], edges[f], new_edges[f]) for f in range(FIELDS)
                ]
                if rights is not None:
                    flux = double_flux(rights, [p[0] for p in pairs])
                    if before is None:
                        bounds.append(flux)
                    else:
                        for f in range(FIELDS):
                            keep(
                                j - 4,
                                f,
                                cells[slot, j - 1, f]
                                - 0.5 * STEP_RATIO * (flux[f] - before[f]),
                            )
                    before = flux
                rights = [p[1] for p in pairs]
            edges = new_edges
        bounds.append(before)
        return bounds

    def group(g, carry):
        base = g * (8 * stride)
        old = [ghosts[pl.ds(pl.multiple_of(f * slots + g * 8, 8), 8), :] for f in range(FIELDS)]
        new = [
            ghosts[pl.ds(pl.multiple_of((FIELDS + f) * slots + g * 8, 8), 8), :]
            for f in range(FIELDS)
        ]
        put_ghosts(0, old)
        put_ghosts(1, [0.5 * (o + n) for o, n in zip(old, new)])
        for x in range(FINE):
            for f in range(FIELDS):
                cells[0, x + 3, f] = fine[pl.ds(base + f * FINE + x, 8, stride=stride), :]

        def keep_middle(x, f, value):
            cells[1, x + 3, f] = value

        active = (lax.broadcasted_iota(jnp.int32, (8, LANES), 0) + g * 8) < live
        final = {}

        def keep_final(x, f, value):
            final[x, f] = value
            fine_out[pl.ds(base + f * FINE + x, 8, stride=stride), :] = jnp.where(
                active, value, 0.0
            )

        first = sweep(0, keep_middle)
        second = sweep(1, keep_final)
        rows = []
        for f in range(FIELDS):
            rows.append(
                fold_four(0.125, *[final[2 * t, f] + final[2 * t + 1, f] for t in range(4)])
            )
        faces = [first[side][f] + second[side][f] for side in range(2) for f in range(FIELDS)]
        faces += [faces[-1], faces[-1]]
        for t in range(3):
            rows.append(fold_four(0.0625, *faces[4 * t : 4 * t + 4]))
        for r, value in enumerate(rows):
            packed[pl.ds(g * 64 + r, 8, stride=BACK_ROWS), :] = value
        return carry

    lax.fori_loop(0, slots // 8, group, 0)

    def put(s, carry):
        @pl.when(s < live)
        def _():
            target = pl.multiple_of(lookups[s] * BACK_ROWS, BACK_ROWS)
            source = pl.multiple_of(s * BACK_ROWS, BACK_ROWS)
            back[pl.ds(target, BACK_ROWS), :] = packed[pl.ds(source, BACK_ROWS), :]

        return carry

    lax.fori_loop(0, slots, put, 0, unroll=4)


def quad_offset(code):
    quad = lax.shift_right_logical(code, 1) & 3
    return lax.shift_right_logical(quad, 1) * 64 + (quad & 1) * 8


def to_quad(value, offset, t):
    return pltpu.roll(value, (offset + LANES - ((t // 2) * 64 + (t % 2) * 8)) & (LANES - 1), 1)


def came_item(came, entry):
    row = lax.shift_right_logical(entry, 7) * BACK_ROWS
    return came[pl.ds(pl.multiple_of(row, BACK_ROWS), BACK_ROWS), :]


def left_kernel(lists, came, face_in, left_out):
    for f in range(FIELDS):
        left_out[f] = jnp.zeros((TILES, LANES), jnp.float32)
    quads = lane_index(1) & 72

    def scatter(n, carry):
        entry = lists[LEFT_ITEMS + n]
        code = entry & (LANES - 1)
        offset = quad_offset(code)
        tile = pl.ds(lax.shift_right_logical(code, 4), 1)
        value = came_item(came, entry)
        moved = [to_quad(value, offset, t) for t in range(4)]
        inside = quads == offset
        for f in range(FIELDS):
            row = FIELDS + f // 4
            fix = STEP_RATIO * (face_in[0, f, tile] - moved[f % 4][row : row + 1])
            left_out[f, tile] = jnp.where(inside, fix, left_out[f, tile])
        return carry

    lax.fori_loop(0, lists[1], scatter, 0)


def merge_kernel(lists, came, swept, face_in, left_in, out, field, cover):
    stride = FIELDS * CELLS
    for i in range(TILES * 2):
        cover[8 * i : 8 * i + 8, :] = jnp.zeros((8, LANES), jnp.float32)
    quads = lane_index(8) & 72

    def scatter(n, carry):
        entry = lists[ALL_ITEMS + n]
        code = entry & (LANES - 1)
        offset = quad_offset(code)
        line = lax.shift_right_logical(code, 3) * 8 + (code & 1) * 4
        value = came_item(came, entry)
        inside = quads == offset
        for t in range(4):
            rows = pl.ds(pl.multiple_of((line + t) * 8, 8), 8)
            field[rows, :] = jnp.where(inside, to_quad(value, offset, t), field[rows, :])
        rows = pl.ds(line, 4)
        cover[rows, :] = jnp.where(inside[:4], 1.0, cover[rows, :])
        return carry

    lax.fori_loop(0, lists[0], scatter, 0)

    for t in range(TILES):
        for e in range(2):
            hit = cover[pl.ds(t * 16 + e * 8, 8), :] > 0.5
            for f in range(FIELDS):
                row = t * stride + f * CELLS + e * 16
                value = field[pl.ds((t * 16 + e * 8) * 8 + f, 8, stride=8), :]
                out[row : row + 8, :] = jnp.where(hit, value, swept[row : row + 8, :])
                out[row + 8 : row + 16, :] = swept[row + 8 : row + 16, :]

    for e, h, start in STARTS:
        line = e * 8 + h * 4
        hit = cover[pl.ds(line, TILES, stride=16), :] > 0.5
        for side in range(2):
            cell = start + 4 if side else start - 1
            if cell < 0:
                continue
            for f in range(FIELDS):
                item = side * FIELDS + f
                face = field[
                    pl.ds((line + item % 4) * 8 + FIELDS + item // 4, TILES, stride=128), :
                ]
                coarse = face_in[FACES.index(start + 4 * side), f]
                fix = STEP_RATIO * ((face - coarse) if side else (coarse - face))
                fix = jnp.where(hit, fix, 0.0)
                rows = pl.ds(f * CELLS + cell, TILES, stride=stride)
                out[rows, :] = out[rows, :] + fix


def last_kernel(incoming, block, out):
    out[...] = block[...]
    for f in range(FIELDS):
        for t in range(TILES):
            out[t, f, 7:8, :] = block[t, f, 7:8, :] + incoming[f, t : t + 1, :]


def in_vmem():
    return pl.BlockSpec(memory_space=pltpu.VMEM)


def in_smem():
    return pl.BlockSpec(memory_space=pltpu.SMEM)


def shaped(*dims):
    return jax.ShapeDtypeStruct(dims, jnp.float32)


def body(coarse_state, fine_state, fine_count, parent_owner, parent_site, fine_half):
    groups = lax.axis_size("gy")
    rows_x = lax.axis_size("gx")
    me = lax.axis_index("gy")
    slots = fine_state.shape[1]
    params = pltpu.CompilerParams(vmem_limit_bytes=VMEM)

    up = [(i, (i + 1) % rows_x) for i in range(rows_x)]
    down = [(j, i) for i, j in up]
    before = lax.ppermute(coarse_state[:, :, CELLS - 8 :], "gx", up)
    after = lax.ppermute(coarse_state[:, :, :8], "gx", down)

    order = jnp.arange(slots, dtype=jnp.int32)
    joined = parent_owner * LANES + parent_site * 2 + fine_half
    joined = joined.reshape(groups, slots)
    active = order[None, :] < fine_count.reshape(groups, 1)
    hit = (lax.shift_right_logical(joined, 7) == me) & active
    key = order[None, :] * LANES + (joined & (LANES - 1))
    big = slots * LANES
    low = jnp.min(jnp.where(hit, key, big), axis=1)
    high = jnp.max(jnp.where(hit, key, -1), axis=1)
    codes = jnp.stack(
        [
            jnp.where(low < big, low & (LANES - 1), -1),
            jnp.where(high > low, high & (LANES - 1), -1),
        ],
        axis=1,
    ).reshape(2 * groups)
    mine = lax.dynamic_index_in_dim(parent_owner.reshape(groups, slots), me, 0, keepdims=False)
    live = lax.dynamic_slice_in_dim(fine_count.reshape(groups), me, 1, 0)
    twin = (mine[:, None] == mine[None, :]) & (order[None, :] < order[:, None])
    lookups = 2 * mine + jnp.any(twin, axis=1).astype(jnp.int32)

    whole = coarse_state.reshape(-1, LANES)
    before = before.reshape(-1, LANES)
    table_shape = shaped(TILES * 16 * GHOST_ROWS, LANES)
    table, kept = pl.pallas_call(
        inner_kernel,
        out_shape=(table_shape, shaped(2, FIELDS, TILES, LANES)),
        in_specs=[in_vmem()],
        out_specs=(in_vmem(), in_vmem()),
        cost_estimate=pl.CostEstimate(flops=4_000_000, bytes_accessed=3_000_000, transcendentals=0),
        compiler_params=params,
        name="inner",
    )(whole)
    table, sending = pl.pallas_call(
        edge_kernel,
        out_shape=(table_shape, shaped(groups, 5, 4, LANES)),
        in_specs=[in_smem(), in_vmem(), in_vmem(), in_vmem(), in_vmem()],
        out_specs=(in_vmem(), in_vmem()),
        input_output_aliases={4: 0},
        compiler_params=params,
        name="edge",
    )(codes, whole, before, kept, table)
    swept, faces, lists = pl.pallas_call(
        coarse_kernel,
        out_shape=(
            shaped(TILES * FIELDS * CELLS, LANES),
            shaped(len(FACES), FIELDS, TILES, LANES),
            jax.ShapeDtypeStruct((512,), jnp.int32),
        ),
        in_specs=[
            in_smem(),
            in_vmem(),
            in_vmem(),
            in_vmem(),
            pl.BlockSpec(memory_space=pl.ANY),
        ],
        out_specs=(in_vmem(), in_vmem(), in_smem()),
        scratch_shapes=[
            pltpu.VMEM((CELLS + 6, FIELDS, TILES, LANES), jnp.float32),
            pltpu.VMEM((CELLS + 1, FIELDS, TILES, LANES), jnp.float32),
        ],
        cost_estimate=pl.CostEstimate(
            flops=10_000_000, bytes_accessed=12_000_000, transcendentals=0
        ),
        compiler_params=params,
        name="coarse",
    )(codes, whole, before, after.reshape(-1, LANES), table)
    arrived = lax.all_to_all(sending, "gy", split_axis=0, concat_axis=0, tiled=True)

    fine_out, back = pl.pallas_call(
        fine_kernel,
        out_shape=(
            shaped(slots * FIELDS * FINE, LANES),
            shaped(groups * 2 * BACK_ROWS, LANES),
        ),
        in_specs=[in_smem(), in_smem(), in_vmem(), in_vmem()],
        out_specs=(in_vmem(), in_vmem()),
        scratch_shapes=[
            pltpu.VMEM((GHOST_ROWS * slots, LANES), jnp.float32),
            pltpu.VMEM((2, FINE + 6, FIELDS, 8, LANES), jnp.float32),
            pltpu.VMEM((slots * BACK_ROWS, LANES), jnp.float32),
        ],
        compiler_params=params,
        name="fine",
    )(lookups, live, arrived, fine_state.reshape(-1, LANES))
    came = lax.all_to_all(
        back.reshape(groups, 2 * BACK_ROWS, LANES), "gy", split_axis=0, concat_axis=0, tiled=True
    )

    came = came.reshape(-1, LANES)
    left_fix = pl.pallas_call(
        left_kernel,
        out_shape=shaped(FIELDS, TILES, LANES),
        in_specs=[in_smem(), in_vmem(), in_vmem()],
        out_specs=in_vmem(),
        compiler_params=params,
        name="left",
    )(lists, came, faces)
    incoming = lax.ppermute(left_fix, "gx", down)
    merged = pl.pallas_call(
        merge_kernel,
        out_shape=shaped(TILES * FIELDS * CELLS, LANES),
        in_specs=[
            in_smem(),
            in_vmem(),
            in_vmem(),
            in_vmem(),
            pl.BlockSpec(memory_space=pl.ANY),
        ],
        out_specs=in_vmem(),
        scratch_shapes=[
            pltpu.VMEM((TILES * 16 * 8, LANES), jnp.float32),
            pltpu.VMEM((TILES * 16, LANES), jnp.float32),
        ],
        cost_estimate=pl.CostEstimate(flops=2_000_000, bytes_accessed=8_000_000, transcendentals=0),
        compiler_params=params,
        name="merge",
    )(lists, came, swept, faces, left_fix)
    spec = pl.BlockSpec((TILES, FIELDS, 8, LANES), lambda i: (0, 0, 3, 0))
    coarse_out = pl.pallas_call(
        last_kernel,
        grid=(1,),
        out_shape=shaped(TILES, FIELDS, CELLS, LANES),
        in_specs=[pl.BlockSpec((FIELDS, TILES, LANES), lambda i: (0, 0, 0)), spec],
        out_specs=spec,
        input_output_aliases={1: 0},
        compiler_params=params,
        name="last",
    )(incoming, merged.reshape(TILES, FIELDS, CELLS, LANES))
    return (coarse_out, fine_out.reshape(fine_state.shape))


def solution(mesh):
    placed = (
        P("gy", None, "gx", None),
        P("gx", "gy", None, None, None),
        P("gx", None),
        P("gx", None),
        P("gx", None),
        P("gx", None),
    )
    return jax.shard_map(
        body,
        mesh=mesh,
        in_specs=placed,
        out_specs=(P("gy", None, "gx", None), P("gx", "gy", None, None, None)),
        check_vma=False,
    )
```

```python
import jax
import jax.numpy as jnp
from jax import lax
from jax.experimental import pallas as pl
from jax.experimental.pallas import tpu as pltpu
from jax.sharding import PartitionSpec as P

SY = 8
SZ = 16
LANES = SY * SZ
FIELDS = 5
TILES = 6
CELLS = 32
FINE = 8
GAMMA = 1.4
STEP_RATIO = 0.1
GHOST_ROWS = 2 * FIELDS
BACK_ROWS = 8
BATCH = 16
STARTS = ((0, 0, 0), (0, 1, 4), (1, 0, 16), (1, 1, 20))
KEPT = (3, 4, 5, 8, 9)
FACES = (0, 4, 8, 16, 20, 24)
MERGE_STEP = 4
ALL_ITEMS = 8
LEFT_ITEMS = 256
VMEM = 48 * 1024 * 1024


def edge_value(outer_left, near_left, near_right, outer_right):
    value = 7.0 / 12.0 * (near_left + near_right) - 1.0 / 12.0 * (outer_left + outer_right)
    low = jnp.minimum(near_left, near_right)
    high = jnp.maximum(near_left, near_right)
    return jnp.minimum(jnp.maximum(value, low), high)


def limit_edges(center, left_edge, right_edge):
    down = center - left_edge
    up = right_edge - center
    twice_down = down + down
    twice_up = up + up
    new_down = jnp.maximum(jnp.minimum(down, twice_up), 0.0) + jnp.minimum(
        jnp.maximum(down, twice_up), 0.0
    )
    new_up = jnp.maximum(jnp.minimum(up, twice_down), 0.0) + jnp.minimum(
        jnp.maximum(up, twice_down), 0.0
    )
    return (center - new_down, center + new_up)


def euler_flux(state):
    density, mom_x, mom_y, mom_z, energy = state
    inverse = 1.0 / density
    velocity = mom_x * inverse
    kinetic = 0.5 * (mom_x * mom_x + mom_y * mom_y + mom_z * mom_z) * inverse
    pressure = (GAMMA - 1.0) * (energy - kinetic)
    fluxes = (
        mom_x,
        mom_x * velocity + pressure,
        mom_y * velocity,
        mom_z * velocity,
        (energy + pressure) * velocity,
    )
    signal = jnp.abs(velocity) + jnp.sqrt(GAMMA * pressure * inverse)
    return (fluxes, signal)


def double_flux(left, right):
    flux_left, signal_left = euler_flux(left)
    flux_right, signal_right = euler_flux(right)
    signal = jnp.maximum(signal_left, signal_right)
    return tuple(
        (fl + fr) - signal * (r - l) for fl, fr, l, r in zip(flux_left, flux_right, left, right)
    )


def lane_index(rows):
    return lax.broadcasted_iota(jnp.int32, (rows, LANES), 1)


def pull_lanes(value, index):
    return jnp.take_along_axis(value, index, axis=1)


def swept_cells(cell, first, last):
    values = {x: cell(x) for x in range(first - 3, last + 4)}
    edges = {}
    for x in range(first - 2, last + 2):
        edges[x] = [
            edge_value(*(values[x + o][f] for o in (-1, 0, 1, 2))) for f in range(FIELDS)
        ]
    limits = {}
    for x in range(first - 1, last + 2):
        limits[x] = [
            limit_edges(values[x][f], edges[x - 1][f], edges[x][f]) for f in range(FIELDS)
        ]
    flux = {}
    for x in range(first, last + 2):
        flux[x] = double_flux([p[1] for p in limits[x - 1]], [p[0] for p in limits[x]])
    return {
        x: [
            values[x][f] - 0.5 * STEP_RATIO * (flux[x + 1][f] - flux[x][f]) for f in range(FIELDS)
        ]
        for x in range(first, last + 1)
    }


def own_cell(own):
    def cell(x):
        return [
            own[pl.ds(f * CELLS + x, TILES, stride=FIELDS * CELLS), :] for f in range(FIELDS)
        ]

    return cell


def write_boxes(table, e, h, old, new):
    lane = lane_index(TILES)
    upper_z = (lane & 8) != 0
    upper_y = (lane & 64) != 0

    def swap(low, high, upper, shift):
        return (
            jnp.where(upper, pltpu.roll(high, shift, 1), low),
            jnp.where(upper, high, pltpu.roll(low, LANES - shift, 1)),
        )

    for age, source in enumerate((old, new)):
        for f in range(FIELDS):
            c0, c1, c2, c3 = [source[o][f] for o in range(4)]
            c0, c1 = swap(c0, c1, upper_z, 8)
            c2, c3 = swap(c2, c3, upper_z, 8)
            c0, c2 = swap(c0, c2, upper_y, 64)
            c1, c3 = swap(c1, c3, upper_y, 64)
            for q, value in enumerate((c0, c1, c2, c3)):
                row = (e * 8 + q * 2 + h) * GHOST_ROWS + age * FIELDS + f
                table[pl.ds(row, TILES, stride=16 * GHOST_ROWS), :] = value


def inner_kernel(own, table, kept):
    cell = own_cell(own)
    new = {}
    for first, last in ((3, 5), (8, 9), (14, 15), (18, 21), (24, 25)):
        new.update(swept_cells(cell, first, last))
    for i, x in enumerate(KEPT):
        for f in range(FIELDS):
            kept[i, f] = new[x][f]
    for e, h, start in STARTS[2:]:
        where = [start + o for o in (-2, -1, 4, 5)]
        write_boxes(table, e, h, [cell(x) for x in where], [new[x] for x in where])


def edge_kernel(codes, own, before, kept, table_in, table, sending):
    inner = own_cell(own)

    def cell(x):
        if x >= 0:
            return inner(x)
        return [before[pl.ds(f * 8 + 8 + x, TILES, stride=FIELDS * 8), :] for f in range(FIELDS)]

    half = 8 * GHOST_ROWS
    for t in range(TILES):
        rows = slice((2 * t + 1) * half, (2 * t + 2) * half)
        table[rows, :] = table_in[rows, :]
    new = swept_cells(cell, -2, -1)
    new.update(swept_cells(cell, 2, 2))
    for i, x in enumerate(KEPT):
        new[x] = [kept[i, f] for f in range(FIELDS)]
    for e, h, start in STARTS[:2]:
        where = [start + o for o in (-2, -1, 4, 5)]
        write_boxes(table, e, h, [cell(x) for x in where], [new[x] for x in where])

    def send(k, carry):
        for c in range(2):
            base = jnp.maximum(codes[2 * k + c], 0) * GHOST_ROWS
            sending[k, 3 * c] = table[pl.ds(base, 4), :]
            sending[k, 3 * c + 1] = table[pl.ds(base + 4, 4), :]
            sending[k, 2, 2 * c : 2 * c + 2] = table[pl.ds(base + 8, 2), :]
        return carry

    lax.fori_loop(0, sending.shape[0], send, 0, unroll=8)


def coarse_kernel(codes, own, before, after, table, swept, face_out, lists, cells, fluxes):
    stride = FIELDS * CELLS
    for f in range(FIELDS):
        for j in range(3):
            cells[j, f] = before[pl.ds(f * 8 + 5 + j, TILES, stride=FIELDS * 8), :]
            cells[35 + j, f] = after[pl.ds(f * 8 + j, TILES, stride=FIELDS * 8), :]

    def load_cells(x, carry):
        for f in range(FIELDS):
            cells[x + 3, f] = own[pl.ds(f * CELLS + x, TILES, stride=stride), :]
        return carry

    lax.fori_loop(0, CELLS, load_cells, 0, unroll=4)

    def limited(j, edge_before):
        edges, lefts, rights = ([], [], [])
        for f in range(FIELDS):
            edge = edge_value(cells[j - 1, f], cells[j, f], cells[j + 1, f], cells[j + 2, f])
            left, right = limit_edges(cells[j, f], edge_before[f], edge)
            edges.append(edge)
            lefts.append(left)
            rights.append(right)
        return (tuple(edges), tuple(lefts), tuple(rights))

    def advance(j, edges, rights):
        edges, lefts, next_rights = limited(j, edges)
        flux = double_flux(rights, lefts)
        for f in range(FIELDS):
            fluxes[j - 3, f] = flux[f]
        return (edges, next_rights, flux)

    edges = tuple(
        edge_value(cells[0, f], cells[1, f], cells[2, f], cells[3, f]) for f in range(FIELDS)
    )
    edges, _, rights = limited(2, edges)
    carry = advance(3, edges, rights)

    def step(x, carry):
        edges, rights, flux_before = carry
        edges, rights, flux = advance(x + 4, edges, rights)
        for f in range(FIELDS):
            swept[pl.ds(f * CELLS + x, TILES, stride=stride), :] = cells[
                x + 3, f
            ] - 0.5 * STEP_RATIO * (flux[f] - flux_before[f])
        return (edges, rights, flux)

    lax.fori_loop(0, CELLS, step, carry, unroll=4)
    for i, face in enumerate(FACES):
        for f in range(FIELDS):
            face_out[i, f] = 0.5 * fluxes[face, f]

    def collect(i, carry):
        total, first = carry
        code = codes[i]
        entry = i * LANES + code
        lists[ALL_ITEMS + total] = entry
        lists[LEFT_ITEMS + first] = entry
        valid = code >= 0
        leftmost = valid & ((code & 9) == 0)
        return (total + valid.astype(jnp.int32), first + leftmost.astype(jnp.int32))

    total, first = lax.fori_loop(0, codes.shape[0], collect, (0, 0), unroll=4)
    for i in range(MERGE_STEP):
        lists[ALL_ITEMS + total + i] = TILES * 16
    lists[0] = lax.shift_right_logical(total + (MERGE_STEP - 1), 2)
    lists[1] = first


def fine_kernel(lookups, arrived, fine, final_out, back, ghosts, cells, packed):
    slots = fine.shape[0] // (FIELDS * FINE)
    stride = FIELDS * FINE
    live = lookups[slots]

    def fetch(s, carry):
        look = lookups[s]
        owner = lax.shift_right_logical(look, 1)
        pos = look & 1
        ghosts[pl.ds(s, 4, stride=slots), :] = arrived[owner, 3 * pos]
        ghosts[pl.ds(s + 4 * slots, 4, stride=slots), :] = arrived[owner, 3 * pos + 1]
        ghosts[pl.ds(s + 8 * slots, 2, stride=slots), :] = arrived[owner, 2, pl.ds(2 * pos, 2)]
        return carry

    lax.fori_loop(0, slots, fetch, 0, unroll=8)

    lane = lane_index(BATCH)
    fine_y = lax.shift_right_logical(lane, 4)
    fine_z = lane & 15
    spread = lax.shift_right_logical(fine_y, 1) * 16 + lax.shift_right_logical(fine_z, 1)
    even_z = (lane & 1) == 0
    even_y = (lane & 16) == 0
    gather_back = (
        (2 * (fine_y & 3) + lax.shift_right_logical(lane, 6)) * 16
        + 2 * (lane & 7)
        + (lax.shift_right_logical(lane, 3) & 1)
    )

    def pair(first, second, even, shift):
        return jnp.where(even, first, pltpu.roll(second, shift, 1)) + jnp.where(
            even, pltpu.roll(first, LANES - shift, 1), second
        )

    def fold_four(scale, a, b, c, d):
        low = pair(a, b, even_z, 1)
        high = pair(c, d, even_z, 1)
        return pull_lanes(scale * pair(low, high, even_y, 16), gather_back)

    def put_ghosts(slot, rows):
        for f in range(FIELDS):
            first, second, third, fourth = [
                pull_lanes(rows[f], spread + (t // 2) * 64 + (t % 2) * 8) for t in range(4)
            ]
            cells[slot, 0, f] = first
            cells[slot, 1, f] = second
            cells[slot, 2, f] = second
            cells[slot, 11, f] = third
            cells[slot, 12, f] = third
            cells[slot, 13, f] = fourth

    def sweep(slot, keep):
        edges = None
        rights = None
        before = None
        bounds = []
        for j in range(1, 12):
            new_edges = [
                edge_value(
                    cells[slot, j - 1, f],
                    cells[slot, j, f],
                    cells[slot, j + 1, f],
                    cells[slot, j + 2, f],
                )
                for f in range(FIELDS)
            ]
            if edges is not None:
                pairs = [
                    limit_edges(cells[slot, j, f], edges[f], new_edges[f]) for f in range(FIELDS)
                ]
                if rights is not None:
                    flux = double_flux(rights, [p[0] for p in pairs])
                    if before is None:
                        bounds.append(flux)
                    else:
                        for f in range(FIELDS):
                            keep(
                                j - 4,
                                f,
                                cells[slot, j - 1, f]
                                - 0.5 * STEP_RATIO * (flux[f] - before[f]),
                            )
                    before = flux
                rights = [p[1] for p in pairs]
            edges = new_edges
        bounds.append(before)
        return bounds

    def group(g, carry):
        base = g * (BATCH * stride)
        rows = [
            ghosts[pl.ds(pl.multiple_of(r * slots + g * BATCH, 8), BATCH), :]
            for r in range(GHOST_ROWS)
        ]
        put_ghosts(0, rows[:FIELDS])
        put_ghosts(1, [0.5 * (o + n) for o, n in zip(rows[:FIELDS], rows[FIELDS:])])
        for x in range(FINE):
            for f in range(FIELDS):
                cells[0, x + 3, f] = fine[pl.ds(base + f * FINE + x, BATCH, stride=stride), :]

        def keep_middle(x, f, value):
            cells[1, x + 3, f] = value

        final = {}

        def keep_final(x, f, value):
            final[x, f] = value
            final_out[pl.ds(base + f * FINE + x, BATCH, stride=stride), :] = value

        first = sweep(0, keep_middle)
        second = sweep(1, keep_final)
        rows = []
        for f in range(FIELDS):
            rows.append(
                fold_four(0.125, *[final[2 * t, f] + final[2 * t + 1, f] for t in range(4)])
            )
        faces = [first[side][f] + second[side][f] for side in range(2) for f in range(FIELDS)]
        faces += [faces[-1], faces[-1]]
        for t in range(3):
            rows.append(fold_four(0.0625, *faces[4 * t : 4 * t + 4]))
        for r, value in enumerate(rows):
            packed[pl.ds(g * (BATCH * BACK_ROWS) + r, BATCH, stride=BACK_ROWS), :] = value
        return carry

    lax.fori_loop(0, slots // BATCH, group, 0)

    def put(s, carry):
        @pl.when(s < live)
        def _():
            target = pl.multiple_of(lookups[s] * BACK_ROWS, BACK_ROWS)
            source = pl.multiple_of(s * BACK_ROWS, BACK_ROWS)
            back[pl.ds(target, BACK_ROWS), :] = packed[pl.ds(source, BACK_ROWS), :]

        return carry

    lax.fori_loop(0, slots, put, 0, unroll=8)


def quad_offset(code):
    quad = lax.shift_right_logical(code, 1) & 3
    return lax.shift_right_logical(quad, 1) * 64 + (quad & 1) * 8


def to_quad(value, offset, t):
    return pltpu.roll(value, (offset + LANES - ((t // 2) * 64 + (t % 2) * 8)) & (LANES - 1), 1)


def came_item(came, entry):
    row = lax.shift_right_logical(entry, 7) * BACK_ROWS
    return came[pl.ds(pl.multiple_of(row, BACK_ROWS), BACK_ROWS), :]


def left_kernel(lists, came, face_in, left_out):
    for f in range(FIELDS):
        left_out[f] = jnp.zeros((TILES, LANES), jnp.float32)
    quads = lane_index(1) & 72

    def scatter(n, carry):
        entry = lists[LEFT_ITEMS + n]
        code = entry & (LANES - 1)
        offset = quad_offset(code)
        tile = pl.ds(lax.shift_right_logical(code, 4), 1)
        value = came_item(came, entry)
        moved = [to_quad(value, offset, t) for t in range(4)]
        inside = quads == offset
        for f in range(FIELDS):
            row = FIELDS + f // 4
            fix = STEP_RATIO * (face_in[0, f, tile] - moved[f % 4][row : row + 1])
            pltpu.store(left_out.at[f, tile], fix, mask=inside)
        return carry

    lax.fori_loop(0, lists[1], scatter, 0)


def merge_kernel(lists, came, swept, face_in, left_in, out, field, cover):
    out[...] = swept[...]
    stride = FIELDS * CELLS
    for i in range(TILES * 2):
        cover[8 * i : 8 * i + 8, :] = jnp.zeros((8, LANES), jnp.float32)
    quads = lane_index(8) & 72

    ones = jnp.ones((4, LANES), jnp.float32)

    def scatter(n, carry):
        for i in range(MERGE_STEP):
            entry = lists[ALL_ITEMS + n * MERGE_STEP + i]
            code = entry & (LANES - 1)
            offset = quad_offset(code)
            line = lax.shift_right_logical(code, 3) * 8 + (code & 1) * 4
            value = came_item(came, entry)
            inside = quads == offset
            for t in range(4):
                rows = pl.ds(pl.multiple_of((line + t) * 8, 8), 8)
                pltpu.store(field.at[rows, :], to_quad(value, offset, t), mask=inside)
            pltpu.store(cover.at[pl.ds(line, 4), :], ones, mask=inside[:4])
        return carry

    lax.fori_loop(0, lists[0], scatter, 0)

    for t in range(TILES):
        for e in range(2):
            hit = cover[pl.ds(t * 16 + e * 8, 8), :] > 0.5
            for f in range(FIELDS):
                row = t * stride + f * CELLS + e * 16
                value = field[pl.ds((t * 16 + e * 8) * 8 + f, 8, stride=8), :]
                pltpu.store(out.at[row : row + 8, :], value, mask=hit)

    for e, h, start in STARTS:
        line = e * 8 + h * 4
        hit = cover[pl.ds(line, TILES, stride=16), :] > 0.5
        for side in range(2):
            cell = start + 4 if side else start - 1
            if cell < 0:
                continue
            for f in range(FIELDS):
                item = side * FIELDS + f
                face = field[
                    pl.ds((line + item % 4) * 8 + FIELDS + item // 4, TILES, stride=128), :
                ]
                coarse = face_in[FACES.index(start + 4 * side), f]
                fix = STEP_RATIO * ((face - coarse) if side else (coarse - face))
                fix = jnp.where(hit, fix, 0.0)
                rows = pl.ds(f * CELLS + cell, TILES, stride=stride)
                out[rows, :] = out[rows, :] + fix


def last_kernel(incoming, merged, out):
    out[...] = merged[...]
    for f in range(FIELDS):
        for t in range(TILES):
            cell = slice(CELLS - 1, CELLS)
            out[t, f, cell, :] = merged[t, f, cell, :] + incoming[f, t : t + 1, :]


def in_vmem():
    return pl.BlockSpec(memory_space=pltpu.VMEM)


def in_smem():
    return pl.BlockSpec(memory_space=pltpu.SMEM)


def shaped(*dims):
    return jax.ShapeDtypeStruct(dims, jnp.float32)


def body(coarse_state, fine_state, fine_count, parent_owner, parent_site, fine_half):
    groups = lax.axis_size("gy")
    rows_x = lax.axis_size("gx")
    me = lax.axis_index("gy")
    slots = fine_state.shape[1]
    params = pltpu.CompilerParams(vmem_limit_bytes=VMEM)

    up = [(i, (i + 1) % rows_x) for i in range(rows_x)]
    down = [(j, i) for i, j in up]
    before = lax.ppermute(coarse_state[:, :, CELLS - 8 :], "gx", up)

    order = jnp.arange(slots, dtype=jnp.int32)
    joined = parent_owner * LANES + parent_site * 2 + fine_half
    joined = joined.reshape(groups, slots)
    active = order[None, :] < fine_count.reshape(groups, 1)
    hit = (lax.shift_right_logical(joined, 7) == me) & active
    key = order[None, :] * LANES + (joined & (LANES - 1))
    big = slots * LANES
    low = jnp.min(jnp.where(hit, key, big), axis=1)
    high = jnp.max(jnp.where(hit, key, -1), axis=1)
    codes = jnp.stack(
        [
            jnp.where(low < big, low & (LANES - 1), -1),
            jnp.where(high > low, high & (LANES - 1), -1),
        ],
        axis=1,
    ).reshape(2 * groups)
    mine = lax.dynamic_index_in_dim(parent_owner.reshape(groups, slots), me, 0, keepdims=False)
    live = lax.dynamic_slice_in_dim(fine_count.reshape(groups), me, 1, 0)
    twin = (mine[:, None] == mine[None, :]) & (order[None, :] < order[:, None])
    lookups = jnp.concatenate([2 * mine + jnp.any(twin, axis=1).astype(jnp.int32), live])

    whole = coarse_state.reshape(-1, LANES)
    before = before.reshape(-1, LANES)
    table_shape = shaped(TILES * 16 * GHOST_ROWS, LANES)
    table, kept = pl.pallas_call(
        inner_kernel,
        out_shape=(table_shape, shaped(len(KEPT), FIELDS, TILES, LANES)),
        in_specs=[in_vmem()],
        out_specs=(in_vmem(), in_vmem()),
        cost_estimate=pl.CostEstimate(flops=4_000_000, bytes_accessed=3_000_000, transcendentals=0),
        compiler_params=params,
        name="inner",
    )(whole)
    table, sending = pl.pallas_call(
        edge_kernel,
        out_shape=(table_shape, shaped(groups, 5, 4, LANES)),
        in_specs=[in_smem(), in_vmem(), in_vmem(), in_vmem(), in_vmem()],
        out_specs=(in_vmem(), in_vmem()),
        compiler_params=params,
        name="edge",
    )(codes, whole, before, kept, table)
    held, table = lax.optimization_barrier((coarse_state, table))
    after = lax.ppermute(held[:, :, :8], "gx", down)
    swept, faces, lists = pl.pallas_call(
        coarse_kernel,
        out_shape=(
            shaped(TILES * FIELDS * CELLS, LANES),
            shaped(len(FACES), FIELDS, TILES, LANES),
            jax.ShapeDtypeStruct((512,), jnp.int32),
        ),
        in_specs=[
            in_smem(),
            in_vmem(),
            in_vmem(),
            in_vmem(),
            pl.BlockSpec(memory_space=pl.ANY),
        ],
        out_specs=(in_vmem(), in_vmem(), in_smem()),
        scratch_shapes=[
            pltpu.VMEM((CELLS + 6, FIELDS, TILES, LANES), jnp.float32),
            pltpu.VMEM((CELLS + 1, FIELDS, TILES, LANES), jnp.float32),
        ],
        cost_estimate=pl.CostEstimate(
            flops=10_000_000, bytes_accessed=12_000_000, transcendentals=0
        ),
        compiler_params=params,
        name="coarse",
    )(codes, whole, before, after.reshape(-1, LANES), table)
    arrived = lax.all_to_all(sending, "gy", split_axis=0, concat_axis=0, tiled=True)

    final, back = pl.pallas_call(
        fine_kernel,
        out_shape=(
            shaped(slots * FIELDS * FINE, LANES),
            shaped(groups * 2 * BACK_ROWS, LANES),
        ),
        in_specs=[in_smem(), in_vmem(), in_vmem()],
        out_specs=(in_vmem(), in_vmem()),
        scratch_shapes=[
            pltpu.VMEM((GHOST_ROWS * slots, LANES), jnp.float32),
            pltpu.VMEM((2, FINE + 6, FIELDS, BATCH, LANES), jnp.float32),
            pltpu.VMEM((slots * BACK_ROWS, LANES), jnp.float32),
        ],
        compiler_params=params,
        name="fine",
    )(lookups, arrived, fine_state.reshape(-1, LANES))
    fine_out = jnp.where(
        (order < live)[:, None, None, None], final.reshape(slots, FIELDS, FINE, LANES), 0.0
    )
    came = lax.all_to_all(
        back.reshape(groups, 2 * BACK_ROWS, LANES), "gy", split_axis=0, concat_axis=0, tiled=True
    )

    came = came.reshape(-1, LANES)
    left_fix = pl.pallas_call(
        left_kernel,
        out_shape=shaped(FIELDS, TILES, LANES),
        in_specs=[in_smem(), in_vmem(), in_vmem()],
        out_specs=in_vmem(),
        compiler_params=params,
        name="left",
    )(lists, came, faces)
    incoming = lax.ppermute(left_fix, "gx", down)
    merged = pl.pallas_call(
        merge_kernel,
        out_shape=shaped(TILES * FIELDS * CELLS, LANES),
        in_specs=[
            in_smem(),
            in_vmem(),
            in_vmem(),
            in_vmem(),
            pl.BlockSpec(memory_space=pl.ANY),
        ],
        out_specs=in_vmem(),
        scratch_shapes=[
            pltpu.VMEM(((TILES * 16 + 8) * 8, LANES), jnp.float32),
            pltpu.VMEM((TILES * 16 + 8, LANES), jnp.float32),
        ],
        cost_estimate=pl.CostEstimate(flops=2_000_000, bytes_accessed=8_000_000, transcendentals=0),
        compiler_params=params,
        name="merge",
    )(lists, came, swept, faces, left_fix)
    coarse_out = pl.pallas_call(
        last_kernel,
        out_shape=shaped(TILES, FIELDS, CELLS, LANES),
        in_specs=[in_vmem(), in_vmem()],
        out_specs=in_vmem(),
        compiler_params=params,
        name="last",
    )(incoming, merged.reshape(TILES, FIELDS, CELLS, LANES))
    return (coarse_out, fine_out.reshape(fine_state.shape))


def solution(mesh):
    placed = (
        P("gy", None, "gx", None),
        P("gx", "gy", None, None, None),
        P("gx", None),
        P("gx", None),
        P("gx", None),
        P("gx", None),
    )
    return jax.shard_map(
        body,
        mesh=mesh,
        in_specs=placed,
        out_specs=(P("gy", None, "gx", None), P("gx", "gy", None, None, None)),
        check_vma=False,
    )
```

```python
import jax
import jax.numpy as jnp
from jax import lax
from jax.experimental import pallas as pl
from jax.experimental.pallas import tpu as pltpu
from jax.sharding import PartitionSpec as P

SY = 8
SZ = 16
LANES = SY * SZ
FIELDS = 5
TILES = 6
CELLS = 32
FINE = 8
GAMMA = 1.4
STEP_RATIO = 0.1
GHOST_ROWS = 2 * FIELDS
BACK_ROWS = 8
BATCH = 16
STARTS = ((0, 0, 0), (0, 1, 4), (1, 0, 16), (1, 1, 20))
KEPT = (3, 4, 5, 8, 9)
FACES = (0, 4, 8, 16, 20, 24)
MERGE_STEP = 4
ALL_ITEMS = 8
LEFT_ITEMS = 256
VMEM = 48 * 1024 * 1024


def edge_value(outer_left, near_left, near_right, outer_right):
    value = 7.0 / 12.0 * (near_left + near_right) - 1.0 / 12.0 * (outer_left + outer_right)
    low = jnp.minimum(near_left, near_right)
    high = jnp.maximum(near_left, near_right)
    return jnp.minimum(jnp.maximum(value, low), high)


def limit_edges(center, left_edge, right_edge):
    down = center - left_edge
    up = right_edge - center
    twice_down = down + down
    twice_up = up + up
    new_down = jnp.maximum(jnp.minimum(down, twice_up), 0.0) + jnp.minimum(
        jnp.maximum(down, twice_up), 0.0
    )
    new_up = jnp.maximum(jnp.minimum(up, twice_down), 0.0) + jnp.minimum(
        jnp.maximum(up, twice_down), 0.0
    )
    return (center - new_down, center + new_up)


def euler_flux(state):
    density, mom_x, mom_y, mom_z, energy = state
    inverse = 1.0 / density
    velocity = mom_x * inverse
    kinetic = 0.5 * (mom_x * mom_x + mom_y * mom_y + mom_z * mom_z) * inverse
    pressure = (GAMMA - 1.0) * (energy - kinetic)
    fluxes = (
        mom_x,
        mom_x * velocity + pressure,
        mom_y * velocity,
        mom_z * velocity,
        (energy + pressure) * velocity,
    )
    signal = jnp.abs(velocity) + jnp.sqrt(GAMMA * pressure * inverse)
    return (fluxes, signal)


def double_flux(left, right):
    flux_left, signal_left = euler_flux(left)
    flux_right, signal_right = euler_flux(right)
    signal = jnp.maximum(signal_left, signal_right)
    return tuple(
        (fl + fr) - signal * (r - l) for fl, fr, l, r in zip(flux_left, flux_right, left, right)
    )


def lane_index(rows):
    return lax.broadcasted_iota(jnp.int32, (rows, LANES), 1)


def pull_lanes(value, index):
    return jnp.take_along_axis(value, index, axis=1)


def swept_cells(cell, first, last):
    values = {x: cell(x) for x in range(first - 3, last + 4)}
    edges = {}
    for x in range(first - 2, last + 2):
        edges[x] = [
            edge_value(*(values[x + o][f] for o in (-1, 0, 1, 2))) for f in range(FIELDS)
        ]
    limits = {}
    for x in range(first - 1, last + 2):
        limits[x] = [
            limit_edges(values[x][f], edges[x - 1][f], edges[x][f]) for f in range(FIELDS)
        ]
    flux = {}
    for x in range(first, last + 2):
        flux[x] = double_flux([p[1] for p in limits[x - 1]], [p[0] for p in limits[x]])
    return {
        x: [
            values[x][f] - 0.5 * STEP_RATIO * (flux[x + 1][f] - flux[x][f]) for f in range(FIELDS)
        ]
        for x in range(first, last + 1)
    }


def own_cell(own):
    def cell(x):
        return [
            own[pl.ds(f * CELLS + x, TILES, stride=FIELDS * CELLS), :] for f in range(FIELDS)
        ]

    return cell


def write_boxes(table, e, h, cells_of_age):
    lane = lane_index(TILES)
    upper_z = (lane & 8) != 0
    upper_y = (lane & 64) != 0

    def swap(low, high, upper, shift):
        return (
            jnp.where(upper, pltpu.roll(high, shift, 1), low),
            jnp.where(upper, high, pltpu.roll(low, LANES - shift, 1)),
        )

    for age, source in cells_of_age.items():
        for f in range(FIELDS):
            c0, c1, c2, c3 = [source[o][f] for o in range(4)]
            c0, c1 = swap(c0, c1, upper_z, 8)
            c2, c3 = swap(c2, c3, upper_z, 8)
            c0, c2 = swap(c0, c2, upper_y, 64)
            c1, c3 = swap(c1, c3, upper_y, 64)
            for q, value in enumerate((c0, c1, c2, c3)):
                row = (e * 8 + q * 2 + h) * GHOST_ROWS + age * FIELDS + f
                table[pl.ds(row, TILES, stride=16 * GHOST_ROWS), :] = value


def load_kernel(
    coarse, owner, site, half, count, own, tail, joined, count_out, tables, sems
):
    rows = FIELDS * CELLS
    loads = [
        pltpu.make_async_copy(ref, tables.at[i], sems.at[TILES + i])
        for i, ref in enumerate((owner, site, half))
    ]
    loads.append(pltpu.make_async_copy(count, count_out, sems.at[TILES + 3]))
    cells = [
        pltpu.make_async_copy(
            coarse.at[t * rows : (t + 1) * rows], own.at[t * rows : (t + 1) * rows], sems.at[t]
        )
        for t in range(TILES)
    ]
    for copy in cells + loads:
        copy.start()
    for t in range(TILES):
        cells[t].wait()
        for f in range(FIELDS):
            i = t * FIELDS + f
            tail[8 * i : 8 * i + 8, :] = own[(i + 1) * CELLS - 8 : (i + 1) * CELLS, :]
    for copy in loads:
        copy.wait()
    joined[...] = tables[0] * LANES + tables[1] * 2 + tables[2]


def inner_kernel(own, table, kept):
    cell = own_cell(own)
    new = {}
    for first, last in ((3, 5), (8, 9), (14, 15), (18, 21), (24, 25)):
        new.update(swept_cells(cell, first, last))
    for i, x in enumerate(KEPT):
        for f in range(FIELDS):
            kept[i, f] = new[x][f]
    for e, h, start in STARTS[1:]:
        where = [start + o for o in (-2, -1, 4, 5)]
        ages = {0: [cell(x) for x in where]}
        if e:
            ages[1] = [new[x] for x in where]
        write_boxes(table, e, h, ages)


def edge_kernel(codes, own, before, kept, table_in, table, sending, staged, sems):
    inner = own_cell(own)

    def cell(x):
        if x >= 0:
            return inner(x)
        return [before[pl.ds(f * 8 + 8 + x, TILES, stride=FIELDS * 8), :] for f in range(FIELDS)]

    table[...] = table_in[...]
    new = swept_cells(cell, -2, -1)
    new.update(swept_cells(cell, 2, 2))
    for i, x in enumerate(KEPT):
        new[x] = [kept[i, f] for f in range(FIELDS)]
    for e, h, start in STARTS[:2]:
        where = [start + o for o in (-2, -1, 4, 5)]
        ages = {1: [new[x] for x in where]}
        if h == 0:
            ages[0] = [cell(x) for x in where]
        write_boxes(table, e, h, ages)

    def send(k, carry):
        for c in range(2):
            base = jnp.maximum(codes[2 * k + c], 0) * GHOST_ROWS
            staged[k, 3 * c] = table[pl.ds(base, 4), :]
            staged[k, 3 * c + 1] = table[pl.ds(base + 4, 4), :]
            staged[k, 2, 2 * c : 2 * c + 2] = table[pl.ds(base + 8, 2), :]
        return carry

    chunks = sems.shape[0]
    size = staged.shape[0] // chunks
    copies = []
    for i in range(chunks):
        lax.fori_loop(i * size, (i + 1) * size, send, 0, unroll=8)
        part = slice(i * size, (i + 1) * size)
        copies.append(pltpu.make_async_copy(staged.at[part], sending.at[part], sems.at[i]))
        copies[-1].start()
    for copy in copies:
        copy.wait()


def coarse_kernel(codes, own, before, after, table, swept, face_out, lists, cells, fluxes):
    stride = FIELDS * CELLS
    for f in range(FIELDS):
        for j in range(3):
            cells[j, f] = before[pl.ds(f * 8 + 5 + j, TILES, stride=FIELDS * 8), :]
            cells[35 + j, f] = after[pl.ds(f * 8 + j, TILES, stride=FIELDS * 8), :]

    def load_cells(x, carry):
        for f in range(FIELDS):
            cells[x + 3, f] = own[pl.ds(f * CELLS + x, TILES, stride=stride), :]
        return carry

    lax.fori_loop(0, CELLS, load_cells, 0, unroll=4)

    def limited(j, edge_before):
        edges, lefts, rights = ([], [], [])
        for f in range(FIELDS):
            edge = edge_value(cells[j - 1, f], cells[j, f], cells[j + 1, f], cells[j + 2, f])
            left, right = limit_edges(cells[j, f], edge_before[f], edge)
            edges.append(edge)
            lefts.append(left)
            rights.append(right)
        return (tuple(edges), tuple(lefts), tuple(rights))

    def advance(j, edges, rights):
        edges, lefts, next_rights = limited(j, edges)
        flux = double_flux(rights, lefts)
        for f in range(FIELDS):
            fluxes[j - 3, f] = flux[f]
        return (edges, next_rights, flux)

    edges = tuple(
        edge_value(cells[0, f], cells[1, f], cells[2, f], cells[3, f]) for f in range(FIELDS)
    )
    edges, _, rights = limited(2, edges)
    carry = advance(3, edges, rights)

    def step(x, carry):
        edges, rights, flux_before = carry
        edges, rights, flux = advance(x + 4, edges, rights)
        for f in range(FIELDS):
            swept[pl.ds(f * CELLS + x, TILES, stride=stride), :] = cells[
                x + 3, f
            ] - 0.5 * STEP_RATIO * (flux[f] - flux_before[f])
        return (edges, rights, flux)

    lax.fori_loop(0, CELLS, step, carry, unroll=4)
    for i, face in enumerate(FACES):
        for f in range(FIELDS):
            face_out[i, f] = 0.5 * fluxes[face, f]

    def collect(i, carry):
        total, first = carry
        code = codes[i]
        entry = i * LANES + code
        lists[ALL_ITEMS + total] = entry
        lists[LEFT_ITEMS + first] = entry
        valid = code >= 0
        leftmost = valid & ((code & 9) == 0)
        return (total + valid.astype(jnp.int32), first + leftmost.astype(jnp.int32))

    total, first = lax.fori_loop(0, codes.shape[0], collect, (0, 0), unroll=4)
    for i in range(MERGE_STEP):
        lists[ALL_ITEMS + total + i] = TILES * 16
        lists[LEFT_ITEMS + first + i] = TILES * 16
    lists[0] = lax.shift_right_logical(total + (MERGE_STEP - 1), 2)
    lists[1] = lax.shift_right_logical(first + (MERGE_STEP - 1), 2)


def fine_kernel(lookups, arrived, fine, final_out, back, ghosts, cells, packed, sems):
    slots = fine.shape[0] // (FIELDS * FINE)
    stride = FIELDS * FINE
    live = lookups[slots]

    def fetch(s, carry):
        look = lookups[s]
        owner = lax.shift_right_logical(look, 1)
        pos = look & 1
        ghosts[pl.ds(s, 4, stride=slots), :] = arrived[owner, 3 * pos]
        ghosts[pl.ds(s + 4 * slots, 4, stride=slots), :] = arrived[owner, 3 * pos + 1]
        ghosts[pl.ds(s + 8 * slots, 2, stride=slots), :] = arrived[owner, 2, pl.ds(2 * pos, 2)]
        return carry

    lax.fori_loop(0, slots, fetch, 0, unroll=8)

    lane = lane_index(BATCH)
    fine_y = lax.shift_right_logical(lane, 4)
    fine_z = lane & 15
    spread = lax.shift_right_logical(fine_y, 1) * 16 + lax.shift_right_logical(fine_z, 1)
    even_z = (lane & 1) == 0
    even_y = (lane & 16) == 0
    gather_back = (
        (2 * (fine_y & 3) + lax.shift_right_logical(lane, 6)) * 16
        + 2 * (lane & 7)
        + (lax.shift_right_logical(lane, 3) & 1)
    )

    def pair(first, second, even, shift):
        return jnp.where(even, first, pltpu.roll(second, shift, 1)) + jnp.where(
            even, pltpu.roll(first, LANES - shift, 1), second
        )

    def fold_four(scale, a, b, c, d):
        low = pair(a, b, even_z, 1)
        high = pair(c, d, even_z, 1)
        return pull_lanes(scale * pair(low, high, even_y, 16), gather_back)

    def put_ghosts(slot, rows):
        for f in range(FIELDS):
            first, second, third, fourth = [
                pull_lanes(rows[f], spread + (t // 2) * 64 + (t % 2) * 8) for t in range(4)
            ]
            cells[slot, 0, f] = first
            cells[slot, 1, f] = second
            cells[slot, 2, f] = second
            cells[slot, 11, f] = third
            cells[slot, 12, f] = third
            cells[slot, 13, f] = fourth

    def sweep(slot, keep):
        edges = None
        rights = None
        before = None
        bounds = []
        for j in range(1, 12):
            new_edges = [
                edge_value(
                    cells[slot, j - 1, f],
                    cells[slot, j, f],
                    cells[slot, j + 1, f],
                    cells[slot, j + 2, f],
                )
                for f in range(FIELDS)
            ]
            if edges is not None:
                pairs = [
                    limit_edges(cells[slot, j, f], edges[f], new_edges[f]) for f in range(FIELDS)
                ]
                if rights is not None:
                    flux = double_flux(rights, [p[0] for p in pairs])
                    if before is None:
                        bounds.append(flux)
                    else:
                        for f in range(FIELDS):
                            keep(
                                j - 4,
                                f,
                                cells[slot, j - 1, f]
                                - 0.5 * STEP_RATIO * (flux[f] - before[f]),
                            )
                    before = flux
                rights = [p[1] for p in pairs]
            edges = new_edges
        bounds.append(before)
        return bounds

    def put(s):
        source = pl.multiple_of(s * BACK_ROWS, BACK_ROWS)
        target = pl.multiple_of(lookups[s] * BACK_ROWS, BACK_ROWS)
        return pltpu.make_async_copy(
            packed.at[pl.ds(source, BACK_ROWS)], back.at[pl.ds(target, BACK_ROWS)], sems.at[s]
        )

    def group(g, carry):
        base = g * (BATCH * stride)
        rows = [
            ghosts[pl.ds(pl.multiple_of(r * slots + g * BATCH, 8), BATCH), :]
            for r in range(GHOST_ROWS)
        ]
        put_ghosts(0, rows[:FIELDS])
        put_ghosts(1, [0.5 * (o + n) for o, n in zip(rows[:FIELDS], rows[FIELDS:])])
        for x in range(FINE):
            for f in range(FIELDS):
                cells[0, x + 3, f] = fine[pl.ds(base + f * FINE + x, BATCH, stride=stride), :]

        def keep_middle(x, f, value):
            cells[1, x + 3, f] = value

        final = {}

        def keep_final(x, f, value):
            final[x, f] = value
            final_out[pl.ds(base + f * FINE + x, BATCH, stride=stride), :] = value

        first = sweep(0, keep_middle)
        second = sweep(1, keep_final)
        rows = []
        for f in range(FIELDS):
            rows.append(
                fold_four(0.125, *[final[2 * t, f] + final[2 * t + 1, f] for t in range(4)])
            )
        faces = [first[side][f] + second[side][f] for side in range(2) for f in range(FIELDS)]
        faces += [faces[-1], faces[-1]]
        for t in range(3):
            rows.append(fold_four(0.0625, *faces[4 * t : 4 * t + 4]))
        for r, value in enumerate(rows):
            packed[pl.ds(g * (BATCH * BACK_ROWS) + r, BATCH, stride=BACK_ROWS), :] = value
        for i in range(BATCH):
            s = g * BATCH + i

            @pl.when(s < live)
            def _():
                put(s).start()

        return carry

    lax.fori_loop(0, slots // BATCH, group, 0)

    def finish(s, carry):
        @pl.when(s < live)
        def _():
            put(s).wait()

        return carry

    lax.fori_loop(0, slots, finish, 0, unroll=8)


def quad_offset(code):
    quad = lax.shift_right_logical(code, 1) & 3
    return lax.shift_right_logical(quad, 1) * 64 + (quad & 1) * 8


def to_quad(value, offset, t):
    return pltpu.roll(value, (offset + LANES - ((t // 2) * 64 + (t % 2) * 8)) & (LANES - 1), 1)


def came_item(came, entry):
    row = lax.shift_right_logical(entry, 7) * BACK_ROWS
    return came[pl.ds(pl.multiple_of(row, BACK_ROWS), BACK_ROWS), :]


def left_kernel(lists, came, face_in, left_out):
    for f in range(FIELDS):
        left_out[f] = jnp.zeros((TILES, LANES), jnp.float32)
    quads = lane_index(1) & 72

    def scatter(n, carry):
        for i in range(MERGE_STEP):
            entry = lists[LEFT_ITEMS + n * MERGE_STEP + i]
            code = entry & (LANES - 1)
            offset = quad_offset(code)
            tile = pl.ds(jnp.minimum(lax.shift_right_logical(code, 4), TILES - 1), 1)
            value = came_item(came, entry)
            moved = [to_quad(value, offset, t) for t in range(4)]
            inside = quads == jnp.where(code < TILES * 16, offset, LANES)
            for f in range(FIELDS):
                row = FIELDS + f // 4
                fix = STEP_RATIO * (face_in[0, f, tile] - moved[f % 4][row : row + 1])
                pltpu.store(left_out.at[f, tile], fix, mask=inside)
        return carry

    lax.fori_loop(0, lists[1], scatter, 0)


def merge_kernel(lists, came, swept, face_in, left_in, out, field, cover):
    out[...] = swept[...]
    stride = FIELDS * CELLS
    for i in range(TILES * 2):
        cover[8 * i : 8 * i + 8, :] = jnp.zeros((8, LANES), jnp.float32)
    quads = lane_index(8) & 72

    ones = jnp.ones((4, LANES), jnp.float32)

    def scatter(n, carry):
        for i in range(MERGE_STEP):
            entry = lists[ALL_ITEMS + n * MERGE_STEP + i]
            code = entry & (LANES - 1)
            offset = quad_offset(code)
            line = lax.shift_right_logical(code, 3) * 8 + (code & 1) * 4
            value = came_item(came, entry)
            inside = quads == offset
            for t in range(4):
                rows = pl.ds(pl.multiple_of((line + t) * 8, 8), 8)
                pltpu.store(field.at[rows, :], to_quad(value, offset, t), mask=inside)
            pltpu.store(cover.at[pl.ds(line, 4), :], ones, mask=inside[:4])
        return carry

    lax.fori_loop(0, lists[0], scatter, 0)

    for t in range(TILES):
        for e in range(2):
            hit = cover[pl.ds(t * 16 + e * 8, 8), :] > 0.5
            for f in range(FIELDS):
                row = t * stride + f * CELLS + e * 16
                value = field[pl.ds((t * 16 + e * 8) * 8 + f, 8, stride=8), :]
                pltpu.store(out.at[row : row + 8, :], value, mask=hit)

    for e, h, start in STARTS:
        line = e * 8 + h * 4
        hit = cover[pl.ds(line, TILES, stride=16), :] > 0.5
        for side in range(2):
            cell = start + 4 if side else start - 1
            if cell < 0:
                continue
            for f in range(FIELDS):
                item = side * FIELDS + f
                face = field[
                    pl.ds((line + item % 4) * 8 + FIELDS + item // 4, TILES, stride=128), :
                ]
                coarse = face_in[FACES.index(start + 4 * side), f]
                fix = STEP_RATIO * ((face - coarse) if side else (coarse - face))
                fix = jnp.where(hit, fix, 0.0)
                rows = pl.ds(f * CELLS + cell, TILES, stride=stride)
                out[rows, :] = out[rows, :] + fix


def last_kernel(incoming, merged, out):
    out[...] = merged[...]
    for f in range(FIELDS):
        for t in range(TILES):
            cell = slice(CELLS - 1, CELLS)
            out[t, f, cell, :] = merged[t, f, cell, :] + incoming[f, t : t + 1, :]


def in_vmem():
    return pl.BlockSpec(memory_space=pltpu.VMEM)


def in_smem():
    return pl.BlockSpec(memory_space=pltpu.SMEM)


def anywhere():
    return pl.BlockSpec(memory_space=pl.ANY)


def shaped(*dims):
    return jax.ShapeDtypeStruct(dims, jnp.float32)


def body(coarse_state, fine_state, fine_count, parent_owner, parent_site, fine_half):
    groups = lax.axis_size("gy")
    rows_x = lax.axis_size("gx")
    me = lax.axis_index("gy")
    slots = fine_state.shape[1]
    params = pltpu.CompilerParams(vmem_limit_bytes=VMEM)

    up = [(i, (i + 1) % rows_x) for i in range(rows_x)]
    down = [(j, i) for i, j in up]
    entries = parent_owner.shape[1]
    whole, tail, joined, counts = pl.pallas_call(
        load_kernel,
        out_shape=(
            shaped(TILES * FIELDS * CELLS, LANES),
            shaped(TILES * FIELDS * 8, LANES),
            jax.ShapeDtypeStruct((1, entries), jnp.int32),
            jax.ShapeDtypeStruct((1, groups), jnp.int32),
        ),
        in_specs=[anywhere()] * 5,
        out_specs=(in_vmem(), in_vmem(), in_vmem(), in_vmem()),
        scratch_shapes=[
            pltpu.VMEM((3, 1, entries), jnp.int32),
            pltpu.SemaphoreType.DMA((TILES + 4,)),
        ],
        compiler_params=params,
        name="load",
    )(coarse_state.reshape(-1, LANES), parent_owner, parent_site, fine_half, fine_count)
    before = lax.ppermute(tail, "gx", up)

    order = jnp.arange(slots, dtype=jnp.int32)
    joined = joined.reshape(groups, slots)
    counts = counts.reshape(groups)
    active = order[None, :] < counts[:, None]
    hit = (lax.shift_right_logical(joined, 7) == me) & active
    key = order[None, :] * LANES + (joined & (LANES - 1))
    big = slots * LANES
    low = jnp.min(jnp.where(hit, key, big), axis=1)
    high = jnp.max(jnp.where(hit, key, -1), axis=1)
    codes = jnp.stack(
        [
            jnp.where(low < big, low & (LANES - 1), -1),
            jnp.where(high > low, high & (LANES - 1), -1),
        ],
        axis=1,
    ).reshape(2 * groups)
    mine = lax.dynamic_index_in_dim(joined, me, 0, keepdims=False)
    mine = lax.shift_right_logical(mine, 7)
    live = lax.dynamic_slice_in_dim(counts, me, 1, 0)
    twin = (mine[:, None] == mine[None, :]) & (order[None, :] < order[:, None])
    lookups = jnp.concatenate([2 * mine + jnp.any(twin, axis=1).astype(jnp.int32), live])

    table_shape = shaped(TILES * 16 * GHOST_ROWS, LANES)
    table, kept = pl.pallas_call(
        inner_kernel,
        out_shape=(table_shape, shaped(len(KEPT), FIELDS, TILES, LANES)),
        in_specs=[in_vmem()],
        out_specs=(in_vmem(), in_vmem()),
        cost_estimate=pl.CostEstimate(flops=4_000_000, bytes_accessed=3_000_000, transcendentals=0),
        compiler_params=params,
        name="inner",
    )(whole)
    table, sending = pl.pallas_call(
        edge_kernel,
        out_shape=(table_shape, shaped(groups, 5, 4, LANES)),
        in_specs=[in_smem(), in_vmem(), in_vmem(), in_vmem(), in_vmem()],
        out_specs=(in_vmem(), anywhere()),
        scratch_shapes=[
            pltpu.VMEM((groups, 5, 4, LANES), jnp.float32),
            pltpu.SemaphoreType.DMA((4,)),
        ],
        compiler_params=params,
        name="edge",
    )(codes, whole, before, kept, table)
    held, table = lax.optimization_barrier((whole, table))
    held = held.reshape(TILES, FIELDS, CELLS, LANES)
    after = lax.ppermute(held[:, :, :8], "gx", down)
    swept, faces, lists = pl.pallas_call(
        coarse_kernel,
        out_shape=(
            shaped(TILES * FIELDS * CELLS, LANES),
            shaped(len(FACES), FIELDS, TILES, LANES),
            jax.ShapeDtypeStruct((512,), jnp.int32),
        ),
        in_specs=[
            in_smem(),
            in_vmem(),
            in_vmem(),
            in_vmem(),
            anywhere(),
        ],
        out_specs=(in_vmem(), in_vmem(), in_smem()),
        scratch_shapes=[
            pltpu.VMEM((CELLS + 6, FIELDS, TILES, LANES), jnp.float32),
            pltpu.VMEM((CELLS + 1, FIELDS, TILES, LANES), jnp.float32),
        ],
        cost_estimate=pl.CostEstimate(
            flops=10_000_000, bytes_accessed=12_000_000, transcendentals=0
        ),
        compiler_params=params,
        name="coarse",
    )(codes, whole, before, after.reshape(-1, LANES), table)
    arrived = lax.all_to_all(sending, "gy", split_axis=0, concat_axis=0, tiled=True)

    final, back = pl.pallas_call(
        fine_kernel,
        out_shape=(
            shaped(slots * FIELDS * FINE, LANES),
            shaped(groups * 2 * BACK_ROWS, LANES),
        ),
        in_specs=[in_smem(), in_vmem(), in_vmem()],
        out_specs=(in_vmem(), anywhere()),
        scratch_shapes=[
            pltpu.VMEM((GHOST_ROWS * slots, LANES), jnp.float32),
            pltpu.VMEM((2, FINE + 6, FIELDS, BATCH, LANES), jnp.float32),
            pltpu.VMEM((slots * BACK_ROWS, LANES), jnp.float32),
            pltpu.SemaphoreType.DMA((slots,)),
        ],
        compiler_params=params,
        name="fine",
    )(lookups, arrived, fine_state.reshape(-1, LANES))
    fine_out = jnp.where(
        (order < live)[:, None, None, None], final.reshape(slots, FIELDS, FINE, LANES), 0.0
    )
    came = lax.all_to_all(
        back.reshape(groups, 2 * BACK_ROWS, LANES), "gy", split_axis=0, concat_axis=0, tiled=True
    )

    came = came.reshape(-1, LANES)
    left_fix = pl.pallas_call(
        left_kernel,
        out_shape=shaped(FIELDS, TILES, LANES),
        in_specs=[in_smem(), in_vmem(), in_vmem()],
        out_specs=in_vmem(),
        compiler_params=params,
        name="left",
    )(lists, came, faces)
    incoming = lax.ppermute(left_fix, "gx", down)
    merged = pl.pallas_call(
        merge_kernel,
        out_shape=shaped(TILES * FIELDS * CELLS, LANES),
        in_specs=[
            in_smem(),
            in_vmem(),
            in_vmem(),
            in_vmem(),
            anywhere(),
        ],
        out_specs=in_vmem(),
        scratch_shapes=[
            pltpu.VMEM(((TILES * 16 + 8) * 8, LANES), jnp.float32),
            pltpu.VMEM((TILES * 16 + 8, LANES), jnp.float32),
        ],
        cost_estimate=pl.CostEstimate(flops=2_000_000, bytes_accessed=8_000_000, transcendentals=0),
        compiler_params=params,
        name="merge",
    )(lists, came, swept, faces, left_fix)
    coarse_out = pl.pallas_call(
        last_kernel,
        out_shape=shaped(TILES, FIELDS, CELLS, LANES),
        in_specs=[in_vmem(), in_vmem()],
        out_specs=in_vmem(),
        compiler_params=params,
        name="last",
    )(incoming, merged.reshape(TILES, FIELDS, CELLS, LANES))
    return (coarse_out, fine_out.reshape(fine_state.shape))


def solution(mesh):
    placed = (
        P("gy", None, "gx", None),
        P("gx", "gy", None, None, None),
        P("gx", None),
        P("gx", None),
        P("gx", None),
        P("gx", None),
    )
    return jax.shard_map(
        body,
        mesh=mesh,
        in_specs=placed,
        out_specs=(P("gy", None, "gx", None), P("gx", "gy", None, None, None)),
        check_vma=False,
    )
```

```python
import jax
import jax.numpy as jnp
from jax import lax
from jax.experimental import pallas as pl
from jax.experimental.pallas import tpu as pltpu
from jax.sharding import PartitionSpec as P

SY = 8
SZ = 16
LANES = SY * SZ
FIELDS = 5
TILES = 6
CELLS = 32
FINE = 8
GAMMA = 1.4
STEP_RATIO = 0.1
GHOST_ROWS = 2 * FIELDS
BACK_ROWS = 8
BATCH = 16
STARTS = ((0, 0, 0), (0, 1, 4), (1, 0, 16), (1, 1, 20))
KEPT = (3, 4, 5, 8, 9)
FACES = (0, 4, 8, 16, 20, 24)
MERGE_STEP = 4
ALL_ITEMS = 8
LEFT_ITEMS = 256
VMEM = 48 * 1024 * 1024


def edge_value(outer_left, near_left, near_right, outer_right):
    value = 7.0 / 12.0 * (near_left + near_right) - 1.0 / 12.0 * (outer_left + outer_right)
    low = jnp.minimum(near_left, near_right)
    high = jnp.maximum(near_left, near_right)
    return jnp.minimum(jnp.maximum(value, low), high)


def limit_edges(center, left_edge, right_edge):
    down = center - left_edge
    up = right_edge - center
    twice_down = down + down
    twice_up = up + up
    new_down = jnp.maximum(jnp.minimum(down, twice_up), 0.0) + jnp.minimum(
        jnp.maximum(down, twice_up), 0.0
    )
    new_up = jnp.maximum(jnp.minimum(up, twice_down), 0.0) + jnp.minimum(
        jnp.maximum(up, twice_down), 0.0
    )
    return (center - new_down, center + new_up)


def euler_flux(state):
    density, mom_x, mom_y, mom_z, energy = state
    inverse = 1.0 / density
    velocity = mom_x * inverse
    kinetic = 0.5 * (mom_x * mom_x + mom_y * mom_y + mom_z * mom_z) * inverse
    pressure = (GAMMA - 1.0) * (energy - kinetic)
    fluxes = (
        mom_x,
        mom_x * velocity + pressure,
        mom_y * velocity,
        mom_z * velocity,
        (energy + pressure) * velocity,
    )
    signal = jnp.abs(velocity) + jnp.sqrt(GAMMA * pressure * inverse)
    return (fluxes, signal)


def double_flux(left, right):
    flux_left, signal_left = euler_flux(left)
    flux_right, signal_right = euler_flux(right)
    signal = jnp.maximum(signal_left, signal_right)
    return tuple(
        (fl + fr) - signal * (r - l) for fl, fr, l, r in zip(flux_left, flux_right, left, right)
    )


def lane_index(rows):
    return lax.broadcasted_iota(jnp.int32, (rows, LANES), 1)


def pull_lanes(value, index):
    return jnp.take_along_axis(value, index, axis=1)


def swept_cells(cell, first, last):
    values = {x: cell(x) for x in range(first - 3, last + 4)}
    edges = {}
    for x in range(first - 2, last + 2):
        edges[x] = [
            edge_value(*(values[x + o][f] for o in (-1, 0, 1, 2))) for f in range(FIELDS)
        ]
    limits = {}
    for x in range(first - 1, last + 2):
        limits[x] = [
            limit_edges(values[x][f], edges[x - 1][f], edges[x][f]) for f in range(FIELDS)
        ]
    flux = {}
    for x in range(first, last + 2):
        flux[x] = double_flux([p[1] for p in limits[x - 1]], [p[0] for p in limits[x]])
    return {
        x: [
            values[x][f] - 0.5 * STEP_RATIO * (flux[x + 1][f] - flux[x][f]) for f in range(FIELDS)
        ]
        for x in range(first, last + 1)
    }


def own_cell(own):
    def cell(x):
        return [
            own[pl.ds(f * CELLS + x, TILES, stride=FIELDS * CELLS), :] for f in range(FIELDS)
        ]

    return cell


def write_boxes(table, e, h, cells_of_age):
    lane = lane_index(TILES)
    upper_z = (lane & 8) != 0
    upper_y = (lane & 64) != 0

    def swap(low, high, upper, shift):
        return (
            jnp.where(upper, pltpu.roll(high, shift, 1), low),
            jnp.where(upper, high, pltpu.roll(low, LANES - shift, 1)),
        )

    for age, source in cells_of_age.items():
        for f in range(FIELDS):
            c0, c1, c2, c3 = [source[o][f] for o in range(4)]
            c0, c1 = swap(c0, c1, upper_z, 8)
            c2, c3 = swap(c2, c3, upper_z, 8)
            c0, c2 = swap(c0, c2, upper_y, 64)
            c1, c3 = swap(c1, c3, upper_y, 64)
            for q, value in enumerate((c0, c1, c2, c3)):
                row = (e * 8 + q * 2 + h) * GHOST_ROWS + age * FIELDS + f
                table[pl.ds(row, TILES, stride=16 * GHOST_ROWS), :] = value


def inner_kernel(own, table, kept):
    cell = own_cell(own)
    new = {}
    for first, last in ((3, 5), (8, 9), (14, 15), (18, 21), (24, 25)):
        new.update(swept_cells(cell, first, last))
    for i, x in enumerate(KEPT):
        for f in range(FIELDS):
            kept[i, f] = new[x][f]
    for e, h, start in STARTS[1:]:
        where = [start + o for o in (-2, -1, 4, 5)]
        ages = {0: [cell(x) for x in where]}
        if e:
            ages[1] = [new[x] for x in where]
        write_boxes(table, e, h, ages)


def edge_kernel(codes, own, before, kept, table_in, table, sending, staged, sems):
    inner = own_cell(own)

    def cell(x):
        if x >= 0:
            return inner(x)
        return [before[pl.ds(f * 8 + 8 + x, TILES, stride=FIELDS * 8), :] for f in range(FIELDS)]

    table[...] = table_in[...]
    new = swept_cells(cell, -2, -1)
    new.update(swept_cells(cell, 2, 2))
    for i, x in enumerate(KEPT):
        new[x] = [kept[i, f] for f in range(FIELDS)]
    for e, h, start in STARTS[:2]:
        where = [start + o for o in (-2, -1, 4, 5)]
        ages = {1: [new[x] for x in where]}
        if h == 0:
            ages[0] = [cell(x) for x in where]
        write_boxes(table, e, h, ages)

    def send(k, carry):
        for c in range(2):
            base = (codes[2 * k + c] & (LANES - 1)) * GHOST_ROWS
            staged[k, 3 * c] = table[pl.ds(base, 4), :]
            staged[k, 3 * c + 1] = table[pl.ds(base + 4, 4), :]
            staged[k, 2, 2 * c : 2 * c + 2] = table[pl.ds(base + 8, 2), :]
        return carry

    chunks = sems.shape[0]
    size = staged.shape[0] // chunks
    copies = []
    for i in range(chunks):
        lax.fori_loop(i * size, (i + 1) * size, send, 0, unroll=8)
        part = slice(i * size, (i + 1) * size)
        copies.append(pltpu.make_async_copy(staged.at[part], sending.at[part], sems.at[i]))
        copies[-1].start()
    for copy in copies:
        copy.wait()


def coarse_kernel(
    codes, counts, live, own, before, after, final, fine_out, swept, face_out, lists, cells, fluxes
):
    size = FIELDS * FINE
    bound = live[0]

    def keep_live(s, carry):
        rows = pl.ds(pl.multiple_of(s * size, size), size)
        fine_out[rows, :] = jnp.where(s < bound, final[rows, :], 0.0)
        return carry

    lax.fori_loop(0, fine_out.shape[0] // size, keep_live, 0, unroll=2)
    stride = FIELDS * CELLS
    for f in range(FIELDS):
        for j in range(3):
            cells[j, f] = before[pl.ds(f * 8 + 5 + j, TILES, stride=FIELDS * 8), :]
            cells[35 + j, f] = after[pl.ds(f * 8 + j, TILES, stride=FIELDS * 8), :]

    def load_cells(x, carry):
        for f in range(FIELDS):
            cells[x + 3, f] = own[pl.ds(f * CELLS + x, TILES, stride=stride), :]
        return carry

    lax.fori_loop(0, CELLS, load_cells, 0, unroll=4)

    def limited(j, edge_before):
        edges, lefts, rights = ([], [], [])
        for f in range(FIELDS):
            edge = edge_value(cells[j - 1, f], cells[j, f], cells[j + 1, f], cells[j + 2, f])
            left, right = limit_edges(cells[j, f], edge_before[f], edge)
            edges.append(edge)
            lefts.append(left)
            rights.append(right)
        return (tuple(edges), tuple(lefts), tuple(rights))

    def advance(j, edges, rights):
        edges, lefts, next_rights = limited(j, edges)
        flux = double_flux(rights, lefts)
        for f in range(FIELDS):
            fluxes[j - 3, f] = flux[f]
        return (edges, next_rights, flux)

    edges = tuple(
        edge_value(cells[0, f], cells[1, f], cells[2, f], cells[3, f]) for f in range(FIELDS)
    )
    edges, _, rights = limited(2, edges)
    carry = advance(3, edges, rights)

    def step(x, carry):
        edges, rights, flux_before = carry
        edges, rights, flux = advance(x + 4, edges, rights)
        for f in range(FIELDS):
            swept[pl.ds(f * CELLS + x, TILES, stride=stride), :] = cells[
                x + 3, f
            ] - 0.5 * STEP_RATIO * (flux[f] - flux_before[f])
        return (edges, rights, flux)

    lax.fori_loop(0, CELLS, step, carry, unroll=4)
    for i, face in enumerate(FACES):
        for f in range(FIELDS):
            face_out[i, f] = 0.5 * fluxes[face, f]

    def collect(i, carry):
        total, first = carry
        code = codes[i] & (LANES - 1)
        entry = i * LANES + code
        lists[ALL_ITEMS + total] = entry
        lists[LEFT_ITEMS + first] = entry
        valid = lax.shift_right_logical(codes[i], 7) < counts[lax.shift_right_logical(i, 1)]
        leftmost = valid & ((code & 9) == 0)
        return (total + valid.astype(jnp.int32), first + leftmost.astype(jnp.int32))

    total, first = lax.fori_loop(0, codes.shape[0], collect, (0, 0), unroll=4)
    for i in range(MERGE_STEP):
        lists[ALL_ITEMS + total + i] = TILES * 16
        lists[LEFT_ITEMS + first + i] = TILES * 16
    lists[0] = lax.shift_right_logical(total + (MERGE_STEP - 1), 2)
    lists[1] = lax.shift_right_logical(first + (MERGE_STEP - 1), 2)


def fine_kernel(lookups, arrived, fine, after, final_out, back, ghosts, cells, packed, sems):
    slots = fine.shape[0] // (FIELDS * FINE)
    stride = FIELDS * FINE
    live = lookups[slots]

    def fetch(s, carry):
        look = lookups[s]
        owner = lax.shift_right_logical(look, 1)
        pos = look & 1
        ghosts[pl.ds(s, 4, stride=slots), :] = arrived[owner, 3 * pos]
        ghosts[pl.ds(s + 4 * slots, 4, stride=slots), :] = arrived[owner, 3 * pos + 1]
        ghosts[pl.ds(s + 8 * slots, 2, stride=slots), :] = arrived[owner, 2, pl.ds(2 * pos, 2)]
        return carry

    lax.fori_loop(0, slots, fetch, 0, unroll=8)

    lane = lane_index(BATCH)
    fine_y = lax.shift_right_logical(lane, 4)
    fine_z = lane & 15
    spread = lax.shift_right_logical(fine_y, 1) * 16 + lax.shift_right_logical(fine_z, 1)
    even_z = (lane & 1) == 0
    even_y = (lane & 16) == 0
    gather_back = (
        (2 * (fine_y & 3) + lax.shift_right_logical(lane, 6)) * 16
        + 2 * (lane & 7)
        + (lax.shift_right_logical(lane, 3) & 1)
    )

    def pair(first, second, even, shift):
        return jnp.where(even, first, pltpu.roll(second, shift, 1)) + jnp.where(
            even, pltpu.roll(first, LANES - shift, 1), second
        )

    def fold_four(scale, a, b, c, d):
        low = pair(a, b, even_z, 1)
        high = pair(c, d, even_z, 1)
        return pull_lanes(scale * pair(low, high, even_y, 16), gather_back)

    def put_ghosts(slot, rows):
        for f in range(FIELDS):
            first, second, third, fourth = [
                pull_lanes(rows[f], spread + (t // 2) * 64 + (t % 2) * 8) for t in range(4)
            ]
            cells[slot, 0, f] = first
            cells[slot, 1, f] = second
            cells[slot, 2, f] = second
            cells[slot, 11, f] = third
            cells[slot, 12, f] = third
            cells[slot, 13, f] = fourth

    def sweep(slot, keep):
        edges = None
        rights = None
        before = None
        bounds = []
        for j in range(1, 12):
            new_edges = [
                edge_value(
                    cells[slot, j - 1, f],
                    cells[slot, j, f],
                    cells[slot, j + 1, f],
                    cells[slot, j + 2, f],
                )
                for f in range(FIELDS)
            ]
            if edges is not None:
                pairs = [
                    limit_edges(cells[slot, j, f], edges[f], new_edges[f]) for f in range(FIELDS)
                ]
                if rights is not None:
                    flux = double_flux(rights, [p[0] for p in pairs])
                    if before is None:
                        bounds.append(flux)
                    else:
                        for f in range(FIELDS):
                            keep(
                                j - 4,
                                f,
                                cells[slot, j - 1, f]
                                - 0.5 * STEP_RATIO * (flux[f] - before[f]),
                            )
                    before = flux
                rights = [p[1] for p in pairs]
            edges = new_edges
        bounds.append(before)
        return bounds

    def put(s):
        source = pl.multiple_of(s * BACK_ROWS, BACK_ROWS)
        target = pl.multiple_of(lookups[s] * BACK_ROWS, BACK_ROWS)
        return pltpu.make_async_copy(
            packed.at[pl.ds(source, BACK_ROWS)], back.at[pl.ds(target, BACK_ROWS)], sems.at[s]
        )

    def group(g, carry):
        base = g * (BATCH * stride)
        rows = [
            ghosts[pl.ds(pl.multiple_of(r * slots + g * BATCH, 8), BATCH), :]
            for r in range(GHOST_ROWS)
        ]
        put_ghosts(0, rows[:FIELDS])
        put_ghosts(1, [0.5 * (o + n) for o, n in zip(rows[:FIELDS], rows[FIELDS:])])
        for x in range(FINE):
            for f in range(FIELDS):
                cells[0, x + 3, f] = fine[pl.ds(base + f * FINE + x, BATCH, stride=stride), :]

        def keep_middle(x, f, value):
            cells[1, x + 3, f] = value

        final = {}

        def keep_final(x, f, value):
            final[x, f] = value
            final_out[pl.ds(base + f * FINE + x, BATCH, stride=stride), :] = value

        first = sweep(0, keep_middle)
        second = sweep(1, keep_final)
        rows = []
        for f in range(FIELDS):
            rows.append(
                fold_four(0.125, *[final[2 * t, f] + final[2 * t + 1, f] for t in range(4)])
            )
        faces = [first[side][f] + second[side][f] for side in range(2) for f in range(FIELDS)]
        faces += [faces[-1], faces[-1]]
        for t in range(3):
            rows.append(fold_four(0.0625, *faces[4 * t : 4 * t + 4]))
        for r, value in enumerate(rows):
            packed[pl.ds(g * (BATCH * BACK_ROWS) + r, BATCH, stride=BACK_ROWS), :] = value
        for i in range(BATCH):
            s = g * BATCH + i

            @pl.when(s < live)
            def _():
                put(s).start()

        return carry

    lax.fori_loop(0, slots // BATCH, group, 0)

    def finish(s, carry):
        @pl.when(s < live)
        def _():
            put(s).wait()

        return carry

    lax.fori_loop(0, slots, finish, 0, unroll=8)


def quad_offset(code):
    quad = lax.shift_right_logical(code, 1) & 3
    return lax.shift_right_logical(quad, 1) * 64 + (quad & 1) * 8


def to_quad(value, offset, t):
    return pltpu.roll(value, (offset + LANES - ((t // 2) * 64 + (t % 2) * 8)) & (LANES - 1), 1)


def came_item(came, entry):
    row = lax.shift_right_logical(entry, 7) * BACK_ROWS
    return came[pl.ds(pl.multiple_of(row, BACK_ROWS), BACK_ROWS), :]


def left_kernel(lists, came, face_in, left_out):
    for f in range(FIELDS):
        left_out[f] = jnp.zeros((TILES, LANES), jnp.float32)
    quads = lane_index(1) & 72

    def scatter(n, carry):
        for i in range(MERGE_STEP):
            entry = lists[LEFT_ITEMS + n * MERGE_STEP + i]
            code = entry & (LANES - 1)
            offset = quad_offset(code)
            tile = pl.ds(jnp.minimum(lax.shift_right_logical(code, 4), TILES - 1), 1)
            value = came_item(came, entry)
            moved = [to_quad(value, offset, t) for t in range(4)]
            inside = quads == jnp.where(code < TILES * 16, offset, LANES)
            for f in range(FIELDS):
                row = FIELDS + f // 4
                fix = STEP_RATIO * (face_in[0, f, tile] - moved[f % 4][row : row + 1])
                pltpu.store(left_out.at[f, tile], fix, mask=inside)
        return carry

    lax.fori_loop(0, lists[1], scatter, 0)


def merge_kernel(lists, came, swept, face_in, left_in, out, field, cover):
    out[...] = swept[...]
    stride = FIELDS * CELLS
    for i in range(TILES * 2):
        cover[8 * i : 8 * i + 8, :] = jnp.zeros((8, LANES), jnp.float32)
    quads = lane_index(8) & 72

    ones = jnp.ones((4, LANES), jnp.float32)

    def scatter(n, carry):
        for i in range(MERGE_STEP):
            entry = lists[ALL_ITEMS + n * MERGE_STEP + i]
            code = entry & (LANES - 1)
            offset = quad_offset(code)
            line = lax.shift_right_logical(code, 3) * 8 + (code & 1) * 4
            value = came_item(came, entry)
            inside = quads == offset
            for t in range(4):
                rows = pl.ds(pl.multiple_of((line + t) * 8, 8), 8)
                pltpu.store(field.at[rows, :], to_quad(value, offset, t), mask=inside)
            pltpu.store(cover.at[pl.ds(line, 4), :], ones, mask=inside[:4])
        return carry

    lax.fori_loop(0, lists[0], scatter, 0)

    for t in range(TILES):
        for e in range(2):
            hit = cover[pl.ds(t * 16 + e * 8, 8), :] > 0.5
            for f in range(FIELDS):
                row = t * stride + f * CELLS + e * 16
                value = field[pl.ds((t * 16 + e * 8) * 8 + f, 8, stride=8), :]
                pltpu.store(out.at[row : row + 8, :], value, mask=hit)

    for e, h, start in STARTS:
        line = e * 8 + h * 4
        hit = cover[pl.ds(line, TILES, stride=16), :] > 0.5
        for side in range(2):
            cell = start + 4 if side else start - 1
            if cell < 0:
                continue
            for f in range(FIELDS):
                item = side * FIELDS + f
                face = field[
                    pl.ds((line + item % 4) * 8 + FIELDS + item // 4, TILES, stride=128), :
                ]
                coarse = face_in[FACES.index(start + 4 * side), f]
                fix = STEP_RATIO * ((face - coarse) if side else (coarse - face))
                fix = jnp.where(hit, fix, 0.0)
                rows = pl.ds(f * CELLS + cell, TILES, stride=stride)
                out[rows, :] = out[rows, :] + fix


def last_kernel(incoming, merged, out):
    out[...] = merged[...]
    for f in range(FIELDS):
        for t in range(TILES):
            cell = slice(CELLS - 1, CELLS)
            out[t, f, cell, :] = merged[t, f, cell, :] + incoming[f, t : t + 1, :]


def in_vmem():
    return pl.BlockSpec(memory_space=pltpu.VMEM)


def in_smem():
    return pl.BlockSpec(memory_space=pltpu.SMEM)


def anywhere():
    return pl.BlockSpec(memory_space=pl.ANY)


def shaped(*dims):
    return jax.ShapeDtypeStruct(dims, jnp.float32)


def body(coarse_state, fine_state, fine_count, parent_owner, parent_site, fine_half):
    groups = lax.axis_size("gy")
    rows_x = lax.axis_size("gx")
    me = lax.axis_index("gy")
    slots = fine_state.shape[1]
    params = pltpu.CompilerParams(vmem_limit_bytes=VMEM)

    up = [(i, (i + 1) % rows_x) for i in range(rows_x)]
    down = [(j, i) for i, j in up]
    before = lax.ppermute(coarse_state[:, :, CELLS - 8 :], "gx", up)
    after = lax.ppermute(coarse_state[:, :, :8], "gx", down)
    whole, before, after = (v.reshape(-1, LANES) for v in (coarse_state, before, after))

    order = jnp.arange(slots, dtype=jnp.int32)
    joined = parent_owner * LANES + parent_site * 2 + fine_half
    joined = joined.reshape(groups, slots)
    hit = lax.shift_right_logical(joined, 7) == me
    key = order[None, :] * LANES + (joined & (LANES - 1))
    key = jnp.where(hit, key, slots * LANES)
    low = jnp.min(key, axis=1)
    next_low = jnp.min(jnp.where(key > low[:, None], key, slots * LANES), axis=1)
    codes = jnp.stack([low, next_low], axis=1).reshape(2 * groups)
    counts = fine_count.reshape(groups)
    mine = lax.dynamic_index_in_dim(joined, me, 0, keepdims=False)
    mine = lax.shift_right_logical(mine, 7)
    live = lax.dynamic_slice_in_dim(counts, me, 1, 0)
    twin = (mine[:, None] == mine[None, :]) & (order[None, :] < order[:, None])
    lookups = jnp.concatenate([2 * mine + jnp.any(twin, axis=1).astype(jnp.int32), live])

    table_shape = shaped(TILES * 16 * GHOST_ROWS, LANES)
    table, kept = pl.pallas_call(
        inner_kernel,
        out_shape=(table_shape, shaped(len(KEPT), FIELDS, TILES, LANES)),
        in_specs=[in_vmem()],
        out_specs=(in_vmem(), in_vmem()),
        cost_estimate=pl.CostEstimate(flops=4_000_000, bytes_accessed=3_000_000, transcendentals=0),
        compiler_params=params,
        name="inner",
    )(whole)
    table, sending = pl.pallas_call(
        edge_kernel,
        out_shape=(table_shape, shaped(groups, 5, 4, LANES)),
        in_specs=[in_smem(), in_vmem(), in_vmem(), in_vmem(), in_vmem()],
        out_specs=(in_vmem(), anywhere()),
        scratch_shapes=[
            pltpu.VMEM((groups, 5, 4, LANES), jnp.float32),
            pltpu.SemaphoreType.DMA((4,)),
        ],
        compiler_params=params,
        name="edge",
    )(codes, whole, before, kept, table)
    arrived = lax.all_to_all(sending, "gy", split_axis=0, concat_axis=0, tiled=True)

    final, back = pl.pallas_call(
        fine_kernel,
        out_shape=(
            shaped(slots * FIELDS * FINE, LANES),
            shaped(groups * 2 * BACK_ROWS, LANES),
        ),
        in_specs=[in_smem(), in_vmem(), in_vmem(), in_vmem()],
        out_specs=(in_vmem(), anywhere()),
        scratch_shapes=[
            pltpu.VMEM((GHOST_ROWS * slots, LANES), jnp.float32),
            pltpu.VMEM((2, FINE + 6, FIELDS, BATCH, LANES), jnp.float32),
            pltpu.VMEM((slots * BACK_ROWS, LANES), jnp.float32),
            pltpu.SemaphoreType.DMA((slots,)),
        ],
        compiler_params=params,
        name="fine",
    )(lookups, arrived, fine_state.reshape(-1, LANES), after)
    fine_out, swept, faces, lists = pl.pallas_call(
        coarse_kernel,
        out_shape=(
            shaped(slots * FIELDS * FINE, LANES),
            shaped(TILES * FIELDS * CELLS, LANES),
            shaped(len(FACES), FIELDS, TILES, LANES),
            jax.ShapeDtypeStruct((512,), jnp.int32),
        ),
        in_specs=[in_smem(), in_smem(), in_smem()] + [in_vmem()] * 4,
        out_specs=(in_vmem(), in_vmem(), in_vmem(), in_smem()),
        scratch_shapes=[
            pltpu.VMEM((CELLS + 6, FIELDS, TILES, LANES), jnp.float32),
            pltpu.VMEM((CELLS + 1, FIELDS, TILES, LANES), jnp.float32),
        ],
        cost_estimate=pl.CostEstimate(
            flops=10_000_000, bytes_accessed=12_000_000, transcendentals=0
        ),
        compiler_params=params,
        name="coarse",
    )(codes, counts, live, whole, before, after, final)
    came = lax.all_to_all(
        back.reshape(groups, 2 * BACK_ROWS, LANES), "gy", split_axis=0, concat_axis=0, tiled=True
    )

    came = came.reshape(-1, LANES)
    left_fix = pl.pallas_call(
        left_kernel,
        out_shape=shaped(FIELDS, TILES, LANES),
        in_specs=[in_smem(), in_vmem(), in_vmem()],
        out_specs=in_vmem(),
        compiler_params=params,
        name="left",
    )(lists, came, faces)
    incoming = lax.ppermute(left_fix, "gx", down)
    merged = pl.pallas_call(
        merge_kernel,
        out_shape=shaped(TILES * FIELDS * CELLS, LANES),
        in_specs=[
            in_smem(),
            in_vmem(),
            in_vmem(),
            in_vmem(),
            anywhere(),
        ],
        out_specs=in_vmem(),
        scratch_shapes=[
            pltpu.VMEM(((TILES * 16 + 8) * 8, LANES), jnp.float32),
            pltpu.VMEM((TILES * 16 + 8, LANES), jnp.float32),
        ],
        cost_estimate=pl.CostEstimate(flops=2_000_000, bytes_accessed=8_000_000, transcendentals=0),
        compiler_params=params,
        name="merge",
    )(lists, came, swept, faces, left_fix)
    coarse_out = pl.pallas_call(
        last_kernel,
        out_shape=shaped(TILES, FIELDS, CELLS, LANES),
        in_specs=[in_vmem(), in_vmem()],
        out_specs=in_vmem(),
        compiler_params=params,
        name="last",
    )(incoming, merged.reshape(TILES, FIELDS, CELLS, LANES))
    return (coarse_out, fine_out.reshape(fine_state.shape))


def solution(mesh):
    placed = (
        P("gy", None, "gx", None),
        P("gx", "gy", None, None, None),
        P("gx", None),
        P("gx", None),
        P("gx", None),
        P("gx", None),
    )
    return jax.shard_map(
        body,
        mesh=mesh,
        in_specs=placed,
        out_specs=(P("gy", None, "gx", None), P("gx", "gy", None, None, None)),
        check_vma=False,
    )
```

```python
import jax
import jax.numpy as jnp
from jax import lax
from jax.experimental import pallas as pl
from jax.experimental.pallas import tpu as pltpu
from jax.sharding import PartitionSpec as P

SY = 8
SZ = 16
LANES = SY * SZ
FIELDS = 5
TILES = 6
CELLS = 32
FINE = 8
GAMMA = 1.4
STEP_RATIO = 0.1
GHOST_ROWS = 2 * FIELDS
BACK_ROWS = 8
BATCH = 16
STARTS = ((0, 0, 0), (0, 1, 4), (1, 0, 16), (1, 1, 20))
KEPT = (3, 4, 5, 8, 9)
FACES = (0, 4, 8, 16, 20, 24)
MERGE_STEP = 4
ALL_ITEMS = 8
LEFT_ITEMS = 256
VMEM = 48 * 1024 * 1024


def edge_value(outer_left, near_left, near_right, outer_right):
    value = 7.0 / 12.0 * (near_left + near_right) - 1.0 / 12.0 * (outer_left + outer_right)
    low = jnp.minimum(near_left, near_right)
    high = jnp.maximum(near_left, near_right)
    return jnp.minimum(jnp.maximum(value, low), high)


def limit_edges(center, left_edge, right_edge):
    down = center - left_edge
    up = right_edge - center
    twice_down = down + down
    twice_up = up + up
    new_down = jnp.minimum(
        jnp.maximum(down, jnp.minimum(twice_up, 0.0)), jnp.maximum(twice_up, 0.0)
    )
    new_up = jnp.minimum(
        jnp.maximum(up, jnp.minimum(twice_down, 0.0)), jnp.maximum(twice_down, 0.0)
    )
    return (center - new_down, center + new_up)


def euler_flux(state):
    density, mom_x, mom_y, mom_z, energy = state
    inverse = 1.0 / density
    velocity = mom_x * inverse
    carried = mom_x * velocity
    kinetic = 0.5 * (carried + (mom_y * mom_y + mom_z * mom_z) * inverse)
    pressure = (GAMMA - 1.0) * (energy - kinetic)
    fluxes = (
        mom_x,
        carried + pressure,
        mom_y * velocity,
        mom_z * velocity,
        (energy + pressure) * velocity,
    )
    signal = jnp.abs(velocity) + jnp.sqrt(GAMMA * pressure * inverse)
    return (fluxes, signal)


def double_flux(left, right):
    flux_left, signal_left = euler_flux(left)
    flux_right, signal_right = euler_flux(right)
    signal = jnp.maximum(signal_left, signal_right)
    return tuple(
        (fl + fr) - signal * (r - l) for fl, fr, l, r in zip(flux_left, flux_right, left, right)
    )


def lane_index(rows):
    return lax.broadcasted_iota(jnp.int32, (rows, LANES), 1)


def pull_lanes(value, index):
    return jnp.take_along_axis(value, index, axis=1)


def swept_cells(cell, first, last):
    values = {x: cell(x) for x in range(first - 3, last + 4)}
    edges = {}
    for x in range(first - 2, last + 2):
        edges[x] = [
            edge_value(*(values[x + o][f] for o in (-1, 0, 1, 2))) for f in range(FIELDS)
        ]
    limits = {}
    for x in range(first - 1, last + 2):
        limits[x] = [
            limit_edges(values[x][f], edges[x - 1][f], edges[x][f]) for f in range(FIELDS)
        ]
    flux = {}
    for x in range(first, last + 2):
        flux[x] = double_flux([p[1] for p in limits[x - 1]], [p[0] for p in limits[x]])
    return {
        x: [
            values[x][f] - 0.5 * STEP_RATIO * (flux[x + 1][f] - flux[x][f]) for f in range(FIELDS)
        ]
        for x in range(first, last + 1)
    }


def own_cell(own):
    def cell(x):
        return [
            own[pl.ds(f * CELLS + x, TILES, stride=FIELDS * CELLS), :] for f in range(FIELDS)
        ]

    return cell


def write_boxes(table, e, h, cells_of_age):
    lane = lane_index(TILES)
    upper_z = (lane & 8) != 0
    upper_y = (lane & 64) != 0

    def swap(low, high, upper, shift):
        return (
            jnp.where(upper, pltpu.roll(high, shift, 1), low),
            jnp.where(upper, high, pltpu.roll(low, LANES - shift, 1)),
        )

    for age, source in cells_of_age.items():
        for f in range(FIELDS):
            c0, c1, c2, c3 = [source[o][f] for o in range(4)]
            c0, c1 = swap(c0, c1, upper_z, 8)
            c2, c3 = swap(c2, c3, upper_z, 8)
            c0, c2 = swap(c0, c2, upper_y, 64)
            c1, c3 = swap(c1, c3, upper_y, 64)
            for q, value in enumerate((c0, c1, c2, c3)):
                row = (e * 8 + q * 2 + h) * GHOST_ROWS + age * FIELDS + f
                table[pl.ds(row, TILES, stride=16 * GHOST_ROWS), :] = value


def inner_kernel(own, table, kept):
    cell = own_cell(own)
    new = {}
    for first, last in ((3, 5), (8, 9), (14, 15), (18, 21), (24, 25)):
        new.update(swept_cells(cell, first, last))
    for i, x in enumerate(KEPT):
        for f in range(FIELDS):
            kept[6 + i, f] = new[x][f]
    for x in range(6):
        for f, value in enumerate(cell(x)):
            kept[x, f] = value
    for e, h, start in STARTS[1:]:
        where = [start + o for o in (-2, -1, 4, 5)]
        ages = {0: [cell(x) for x in where]}
        if e:
            ages[1] = [new[x] for x in where]
        write_boxes(table, e, h, ages)


def edge_kernel(codes, before, kept, table_in, table, sending, staged, sems):
    def cell(x):
        if x >= 0:
            return [kept[x, f] for f in range(FIELDS)]
        return [before[pl.ds(f * 8 + 8 + x, TILES, stride=FIELDS * 8), :] for f in range(FIELDS)]

    table[...] = table_in[...]
    new = swept_cells(cell, -2, -1)
    new.update(swept_cells(cell, 2, 2))
    for i, x in enumerate(KEPT):
        new[x] = [kept[6 + i, f] for f in range(FIELDS)]
    for e, h, start in STARTS[:2]:
        where = [start + o for o in (-2, -1, 4, 5)]
        ages = {1: [new[x] for x in where]}
        if h == 0:
            ages[0] = [cell(x) for x in where]
        write_boxes(table, e, h, ages)

    def send(k, carry):
        for c in range(2):
            base = (codes[2 * k + c] & (LANES - 1)) * GHOST_ROWS
            staged[k, 3 * c] = table[pl.ds(base, 4), :]
            staged[k, 3 * c + 1] = table[pl.ds(base + 4, 4), :]
            staged[k, 2, 2 * c : 2 * c + 2] = table[pl.ds(base + 8, 2), :]
        return carry

    chunks = sems.shape[0]
    size = staged.shape[0] // chunks
    copies = []
    for i in range(chunks):
        lax.fori_loop(i * size, (i + 1) * size, send, 0, unroll=8)
        part = slice(i * size, (i + 1) * size)
        copies.append(pltpu.make_async_copy(staged.at[part], sending.at[part], sems.at[i]))
        copies[-1].start()
    for copy in copies:
        copy.wait()


def coarse_kernel(
    codes, counts, live, own, before, after, final, fine_out, swept, face_out, lists, cells, fluxes
):
    size = FIELDS * FINE
    bound = live[0]

    def keep_live(s, carry):
        rows = pl.ds(pl.multiple_of(s * size, size), size)
        fine_out[rows, :] = jnp.where(s < bound, final[rows, :], 0.0)
        return carry

    lax.fori_loop(0, fine_out.shape[0] // size, keep_live, 0, unroll=2)
    stride = FIELDS * CELLS
    for f in range(FIELDS):
        for j in range(3):
            cells[j, f] = before[pl.ds(f * 8 + 5 + j, TILES, stride=FIELDS * 8), :]
            cells[35 + j, f] = after[pl.ds(f * 8 + j, TILES, stride=FIELDS * 8), :]

    def load_cells(x, carry):
        for f in range(FIELDS):
            cells[x + 3, f] = own[pl.ds(f * CELLS + x, TILES, stride=stride), :]
        return carry

    lax.fori_loop(0, CELLS, load_cells, 0, unroll=4)

    def limited(j, edge_before):
        edges, lefts, rights = ([], [], [])
        for f in range(FIELDS):
            edge = edge_value(cells[j - 1, f], cells[j, f], cells[j + 1, f], cells[j + 2, f])
            left, right = limit_edges(cells[j, f], edge_before[f], edge)
            edges.append(edge)
            lefts.append(left)
            rights.append(right)
        return (tuple(edges), tuple(lefts), tuple(rights))

    def advance(j, edges, rights):
        edges, lefts, next_rights = limited(j, edges)
        flux = double_flux(rights, lefts)
        for f in range(FIELDS):
            fluxes[j - 3, f] = flux[f]
        return (edges, next_rights, flux)

    edges = tuple(
        edge_value(cells[0, f], cells[1, f], cells[2, f], cells[3, f]) for f in range(FIELDS)
    )
    edges, _, rights = limited(2, edges)
    carry = advance(3, edges, rights)

    def step(x, carry):
        edges, rights, flux_before = carry
        edges, rights, flux = advance(x + 4, edges, rights)
        for f in range(FIELDS):
            swept[pl.ds(f * CELLS + x, TILES, stride=stride), :] = cells[
                x + 3, f
            ] - 0.5 * STEP_RATIO * (flux[f] - flux_before[f])
        return (edges, rights, flux)

    lax.fori_loop(0, CELLS, step, carry, unroll=4)
    for i, face in enumerate(FACES):
        for f in range(FIELDS):
            face_out[i, f] = 0.5 * fluxes[face, f]

    def collect(i, carry):
        total, first = carry
        code = codes[i] & (LANES - 1)
        entry = i * LANES + code
        lists[ALL_ITEMS + total] = entry
        lists[LEFT_ITEMS + first] = entry
        valid = lax.shift_right_logical(codes[i], 7) < counts[lax.shift_right_logical(i, 1)]
        leftmost = valid & ((code & 9) == 0)
        return (total + valid.astype(jnp.int32), first + leftmost.astype(jnp.int32))

    total, first = lax.fori_loop(0, codes.shape[0], collect, (0, 0), unroll=4)
    for i in range(MERGE_STEP):
        lists[ALL_ITEMS + total + i] = TILES * 16
        lists[LEFT_ITEMS + first + i] = TILES * 16
    lists[0] = lax.shift_right_logical(total + (MERGE_STEP - 1), 2)
    lists[1] = lax.shift_right_logical(first + (MERGE_STEP - 1), 2)


def fine_kernel(lookups, arrived, fine, after, final_out, back, ghosts, cells, packed, sems):
    slots = fine.shape[0] // (FIELDS * FINE)
    stride = FIELDS * FINE
    live = lookups[slots]

    def fetch(s, carry):
        look = lookups[s]
        owner = lax.shift_right_logical(look, 1)
        pos = look & 1
        ghosts[pl.ds(s, 4, stride=slots), :] = arrived[owner, 3 * pos]
        ghosts[pl.ds(s + 4 * slots, 4, stride=slots), :] = arrived[owner, 3 * pos + 1]
        ghosts[pl.ds(s + 8 * slots, 2, stride=slots), :] = arrived[owner, 2, pl.ds(2 * pos, 2)]
        return carry

    lax.fori_loop(0, slots, fetch, 0, unroll=8)

    lane = lane_index(BATCH)
    fine_y = lax.shift_right_logical(lane, 4)
    fine_z = lane & 15
    spread = lax.shift_right_logical(fine_y, 1) * 16 + lax.shift_right_logical(fine_z, 1)
    even_z = (lane & 1) == 0
    even_y = (lane & 16) == 0
    gather_back = (
        (2 * (fine_y & 3) + lax.shift_right_logical(lane, 6)) * 16
        + 2 * (lane & 7)
        + (lax.shift_right_logical(lane, 3) & 1)
    )

    def pair(first, second, even, shift):
        return jnp.where(even, first, pltpu.roll(second, shift, 1)) + jnp.where(
            even, pltpu.roll(first, LANES - shift, 1), second
        )

    def fold_four(scale, a, b, c, d):
        low = pair(a, b, even_z, 1)
        high = pair(c, d, even_z, 1)
        return pull_lanes(scale * pair(low, high, even_y, 16), gather_back)

    def put_ghosts(slot, rows):
        for f in range(FIELDS):
            first, second, third, fourth = [
                pull_lanes(rows[f], spread + (t // 2) * 64 + (t % 2) * 8) for t in range(4)
            ]
            cells[slot, 0, f] = first
            cells[slot, 1, f] = second
            cells[slot, 2, f] = second
            cells[slot, 11, f] = third
            cells[slot, 12, f] = third
            cells[slot, 13, f] = fourth

    def sweep(slot, keep):
        edges = None
        rights = None
        before = None
        bounds = []
        for j in range(1, 12):
            new_edges = [
                edge_value(
                    cells[slot, j - 1, f],
                    cells[slot, j, f],
                    cells[slot, j + 1, f],
                    cells[slot, j + 2, f],
                )
                for f in range(FIELDS)
            ]
            if edges is not None:
                pairs = [
                    limit_edges(cells[slot, j, f], edges[f], new_edges[f]) for f in range(FIELDS)
                ]
                if rights is not None:
                    flux = double_flux(rights, [p[0] for p in pairs])
                    if before is None:
                        bounds.append(flux)
                    else:
                        for f in range(FIELDS):
                            keep(
                                j - 4,
                                f,
                                cells[slot, j - 1, f]
                                - 0.5 * STEP_RATIO * (flux[f] - before[f]),
                            )
                    before = flux
                rights = [p[1] for p in pairs]
            edges = new_edges
        bounds.append(before)
        return bounds

    def put(s):
        source = pl.multiple_of(s * BACK_ROWS, BACK_ROWS)
        target = pl.multiple_of(lookups[s] * BACK_ROWS, BACK_ROWS)
        return pltpu.make_async_copy(
            packed.at[pl.ds(source, BACK_ROWS)], back.at[pl.ds(target, BACK_ROWS)], sems.at[s]
        )

    def group(g, carry):
        base = g * (BATCH * stride)
        rows = [
            ghosts[pl.ds(pl.multiple_of(r * slots + g * BATCH, 8), BATCH), :]
            for r in range(GHOST_ROWS)
        ]
        put_ghosts(0, rows[:FIELDS])
        put_ghosts(1, [0.5 * (o + n) for o, n in zip(rows[:FIELDS], rows[FIELDS:])])
        for x in range(FINE):
            for f in range(FIELDS):
                cells[0, x + 3, f] = fine[pl.ds(base + f * FINE + x, BATCH, stride=stride), :]

        def keep_middle(x, f, value):
            cells[1, x + 3, f] = value

        final = {}

        def keep_final(x, f, value):
            final[x, f] = value
            final_out[pl.ds(base + f * FINE + x, BATCH, stride=stride), :] = value

        first = sweep(0, keep_middle)
        second = sweep(1, keep_final)
        rows = []
        for f in range(FIELDS):
            rows.append(
                fold_four(0.125, *[final[2 * t, f] + final[2 * t + 1, f] for t in range(4)])
            )
        faces = [first[side][f] + second[side][f] for side in range(2) for f in range(FIELDS)]
        faces += [faces[-1], faces[-1]]
        for t in range(3):
            rows.append(fold_four(0.0625, *faces[4 * t : 4 * t + 4]))
        for r, value in enumerate(rows):
            packed[pl.ds(g * (BATCH * BACK_ROWS) + r, BATCH, stride=BACK_ROWS), :] = value
        for i in range(BATCH):
            s = g * BATCH + i

            @pl.when(s < live)
            def _():
                put(s).start()

        return carry

    lax.fori_loop(0, slots // BATCH, group, 0)

    def finish(s, carry):
        @pl.when(s < live)
        def _():
            put(s).wait()

        return carry

    lax.fori_loop(0, slots, finish, 0, unroll=8)


def quad_offset(code):
    quad = lax.shift_right_logical(code, 1) & 3
    return lax.shift_right_logical(quad, 1) * 64 + (quad & 1) * 8


def to_quad(value, offset, t):
    return pltpu.roll(value, (offset + LANES - ((t // 2) * 64 + (t % 2) * 8)) & (LANES - 1), 1)


def came_item(came, entry):
    row = lax.shift_right_logical(entry, 7) * BACK_ROWS
    return came[pl.ds(pl.multiple_of(row, BACK_ROWS), BACK_ROWS), :]


def left_kernel(lists, came, face_in, left_out):
    for f in range(FIELDS):
        left_out[f] = jnp.zeros((TILES, LANES), jnp.float32)
    quads = lane_index(1) & 72

    def scatter(n, carry):
        for i in range(MERGE_STEP):
            entry = lists[LEFT_ITEMS + n * MERGE_STEP + i]
            code = entry & (LANES - 1)
            offset = quad_offset(code)
            tile = pl.ds(jnp.minimum(lax.shift_right_logical(code, 4), TILES - 1), 1)
            value = came_item(came, entry)
            moved = [to_quad(value, offset, t) for t in range(4)]
            inside = quads == jnp.where(code < TILES * 16, offset, LANES)
            for f in range(FIELDS):
                row = FIELDS + f // 4
                fix = STEP_RATIO * (face_in[0, f, tile] - moved[f % 4][row : row + 1])
                pltpu.store(left_out.at[f, tile], fix, mask=inside)
        return carry

    lax.fori_loop(0, lists[1], scatter, 0)


def merge_kernel(lists, came, swept, face_in, left_in, out, field, cover):
    out[...] = swept[...]
    stride = FIELDS * CELLS
    for i in range(TILES * 2):
        cover[8 * i : 8 * i + 8, :] = jnp.zeros((8, LANES), jnp.float32)
    quads = lane_index(8) & 72

    ones = jnp.ones((4, LANES), jnp.float32)

    def scatter(n, carry):
        for i in range(MERGE_STEP):
            entry = lists[ALL_ITEMS + n * MERGE_STEP + i]
            code = entry & (LANES - 1)
            offset = quad_offset(code)
            line = lax.shift_right_logical(code, 3) * 8 + (code & 1) * 4
            value = came_item(came, entry)
            inside = quads == offset
            for t in range(4):
                rows = pl.ds(pl.multiple_of((line + t) * 8, 8), 8)
                pltpu.store(field.at[rows, :], to_quad(value, offset, t), mask=inside)
            pltpu.store(cover.at[pl.ds(line, 4), :], ones, mask=inside[:4])
        return carry

    lax.fori_loop(0, lists[0], scatter, 0)

    for t in range(TILES):
        for e in range(2):
            hit = cover[pl.ds(t * 16 + e * 8, 8), :] > 0.5
            for f in range(FIELDS):
                row = t * stride + f * CELLS + e * 16
                value = field[pl.ds((t * 16 + e * 8) * 8 + f, 8, stride=8), :]
                pltpu.store(out.at[row : row + 8, :], value, mask=hit)

    for e, h, start in STARTS:
        line = e * 8 + h * 4
        hit = cover[pl.ds(line, TILES, stride=16), :] > 0.5
        for side in range(2):
            cell = start + 4 if side else start - 1
            if cell < 0:
                continue
            for f in range(FIELDS):
                item = side * FIELDS + f
                face = field[
                    pl.ds((line + item % 4) * 8 + FIELDS + item // 4, TILES, stride=128), :
                ]
                coarse = face_in[FACES.index(start + 4 * side), f]
                fix = STEP_RATIO * ((face - coarse) if side else (coarse - face))
                fix = jnp.where(hit, fix, 0.0)
                rows = pl.ds(f * CELLS + cell, TILES, stride=stride)
                out[rows, :] = out[rows, :] + fix


def last_kernel(incoming, merged, out):
    out[...] = merged[...]
    for f in range(FIELDS):
        for t in range(TILES):
            cell = slice(CELLS - 1, CELLS)
            out[t, f, cell, :] = merged[t, f, cell, :] + incoming[f, t : t + 1, :]


def in_vmem():
    return pl.BlockSpec(memory_space=pltpu.VMEM)


def in_smem():
    return pl.BlockSpec(memory_space=pltpu.SMEM)


def anywhere():
    return pl.BlockSpec(memory_space=pl.ANY)


def shaped(*dims):
    return jax.ShapeDtypeStruct(dims, jnp.float32)


def body(coarse_state, fine_state, fine_count, parent_owner, parent_site, fine_half):
    groups = lax.axis_size("gy")
    rows_x = lax.axis_size("gx")
    me = lax.axis_index("gy")
    slots = fine_state.shape[1]
    params = pltpu.CompilerParams(vmem_limit_bytes=VMEM)

    up = [(i, (i + 1) % rows_x) for i in range(rows_x)]
    down = [(j, i) for i, j in up]
    before = lax.ppermute(coarse_state[:, :, CELLS - 8 :], "gx", up)
    after = lax.ppermute(coarse_state[:, :, :8], "gx", down)
    whole, before, after = (v.reshape(-1, LANES) for v in (coarse_state, before, after))

    order = jnp.arange(slots, dtype=jnp.int32)
    joined = parent_owner * LANES + parent_site * 2 + fine_half
    joined = joined.reshape(groups, slots)
    hit = lax.shift_right_logical(joined, 7) == me
    key = order[None, :] * LANES + (joined & (LANES - 1))
    key = jnp.where(hit, key, slots * LANES)
    low = jnp.min(key, axis=1)
    next_low = jnp.min(jnp.where(key > low[:, None], key, slots * LANES), axis=1)
    codes = jnp.stack([low, next_low], axis=1).reshape(2 * groups)
    counts = fine_count.reshape(groups)
    mine = lax.dynamic_index_in_dim(joined, me, 0, keepdims=False)
    mine = lax.shift_right_logical(mine, 7)
    live = lax.dynamic_slice_in_dim(counts, me, 1, 0)
    twin = (mine[:, None] == mine[None, :]) & (order[None, :] < order[:, None])
    lookups = jnp.concatenate([2 * mine + jnp.any(twin, axis=1).astype(jnp.int32), live])

    table_shape = shaped(TILES * 16 * GHOST_ROWS, LANES)
    table, kept = pl.pallas_call(
        inner_kernel,
        out_shape=(table_shape, shaped(6 + len(KEPT), FIELDS, TILES, LANES)),
        in_specs=[in_vmem()],
        out_specs=(in_vmem(), in_vmem()),
        cost_estimate=pl.CostEstimate(flops=4_000_000, bytes_accessed=3_000_000, transcendentals=0),
        compiler_params=params,
        name="inner",
    )(whole)
    table, sending = pl.pallas_call(
        edge_kernel,
        out_shape=(table_shape, shaped(groups, 5, 4, LANES)),
        in_specs=[in_smem(), in_vmem(), in_vmem(), in_vmem()],
        out_specs=(in_vmem(), anywhere()),
        scratch_shapes=[
            pltpu.VMEM((groups, 5, 4, LANES), jnp.float32),
            pltpu.SemaphoreType.DMA((4,)),
        ],
        compiler_params=params,
        name="edge",
    )(codes, before, kept, table)
    arrived = lax.all_to_all(sending, "gy", split_axis=0, concat_axis=0, tiled=True)

    final, back = pl.pallas_call(
        fine_kernel,
        out_shape=(
            shaped(slots * FIELDS * FINE, LANES),
            shaped(groups * 2 * BACK_ROWS, LANES),
        ),
        in_specs=[in_smem(), in_vmem(), in_vmem(), in_vmem()],
        out_specs=(in_vmem(), anywhere()),
        scratch_shapes=[
            pltpu.VMEM((GHOST_ROWS * slots, LANES), jnp.float32),
            pltpu.VMEM((2, FINE + 6, FIELDS, BATCH, LANES), jnp.float32),
            pltpu.VMEM((slots * BACK_ROWS, LANES), jnp.float32),
            pltpu.SemaphoreType.DMA((slots,)),
        ],
        compiler_params=params,
        name="fine",
    )(lookups, arrived, fine_state.reshape(-1, LANES), after)
    fine_out, swept, faces, lists = pl.pallas_call(
        coarse_kernel,
        out_shape=(
            shaped(slots * FIELDS * FINE, LANES),
            shaped(TILES * FIELDS * CELLS, LANES),
            shaped(len(FACES), FIELDS, TILES, LANES),
            jax.ShapeDtypeStruct((512,), jnp.int32),
        ),
        in_specs=[in_smem(), in_smem(), in_smem()] + [in_vmem()] * 4,
        out_specs=(in_vmem(), in_vmem(), in_vmem(), in_smem()),
        scratch_shapes=[
            pltpu.VMEM((CELLS + 6, FIELDS, TILES, LANES), jnp.float32),
            pltpu.VMEM((CELLS + 1, FIELDS, TILES, LANES), jnp.float32),
        ],
        cost_estimate=pl.CostEstimate(
            flops=10_000_000, bytes_accessed=12_000_000, transcendentals=0
        ),
        compiler_params=params,
        name="coarse",
    )(codes, counts, live, whole, before, after, final)
    came = lax.all_to_all(
        back.reshape(groups, 2 * BACK_ROWS, LANES), "gy", split_axis=0, concat_axis=0, tiled=True
    )

    came = came.reshape(-1, LANES)
    left_fix = pl.pallas_call(
        left_kernel,
        out_shape=shaped(FIELDS, TILES, LANES),
        in_specs=[in_smem(), in_vmem(), in_vmem()],
        out_specs=in_vmem(),
        compiler_params=params,
        name="left",
    )(lists, came, faces)
    incoming = lax.ppermute(left_fix, "gx", down)
    merged = pl.pallas_call(
        merge_kernel,
        out_shape=shaped(TILES * FIELDS * CELLS, LANES),
        in_specs=[
            in_smem(),
            in_vmem(),
            in_vmem(),
            in_vmem(),
            anywhere(),
        ],
        out_specs=in_vmem(),
        scratch_shapes=[
            pltpu.VMEM(((TILES * 16 + 8) * 8, LANES), jnp.float32),
            pltpu.VMEM((TILES * 16 + 8, LANES), jnp.float32),
        ],
        cost_estimate=pl.CostEstimate(flops=2_000_000, bytes_accessed=8_000_000, transcendentals=0),
        compiler_params=params,
        name="merge",
    )(lists, came, swept, faces, left_fix)
    coarse_out = pl.pallas_call(
        last_kernel,
        out_shape=shaped(TILES, FIELDS, CELLS, LANES),
        in_specs=[in_vmem(), in_vmem()],
        out_specs=in_vmem(),
        compiler_params=params,
        name="last",
    )(incoming, merged.reshape(TILES, FIELDS, CELLS, LANES))
    return (coarse_out, fine_out.reshape(fine_state.shape))


def solution(mesh):
    placed = (
        P("gy", None, "gx", None),
        P("gx", "gy", None, None, None),
        P("gx", None),
        P("gx", None),
        P("gx", None),
        P("gx", None),
    )
    return jax.shard_map(
        body,
        mesh=mesh,
        in_specs=placed,
        out_specs=(P("gy", None, "gx", None), P("gx", "gy", None, None, None)),
        check_vma=False,
    )
```

```python
import jax
import jax.numpy as jnp
from jax import lax
from jax.experimental import pallas as pl
from jax.experimental.pallas import tpu as pltpu
from jax.sharding import PartitionSpec as P

SY = 8
SZ = 16
LANES = SY * SZ
FIELDS = 5
TILES = 6
CELLS = 32
FINE = 8
GAMMA = 1.4
STEP_RATIO = 0.1
GHOST_ROWS = 2 * FIELDS
BACK_ROWS = 8
BATCH = 16
STARTS = ((0, 0, 0), (0, 1, 4), (1, 0, 16), (1, 1, 20))
KEPT = (3, 4, 5, 8, 9)
FACES = (0, 4, 8, 16, 20, 24)
MERGE_STEP = 4
ALL_ITEMS = 8
LEFT_ITEMS = 256
VMEM = 48 * 1024 * 1024


def edge_value(outer_left, near_left, near_right, outer_right):
    value = 7.0 / 12.0 * (near_left + near_right) - 1.0 / 12.0 * (outer_left + outer_right)
    low = jnp.minimum(near_left, near_right)
    high = jnp.maximum(near_left, near_right)
    return jnp.minimum(jnp.maximum(value, low), high)


def limit_edges(center, left_edge, right_edge):
    down = center - left_edge
    up = right_edge - center
    twice_down = down + down
    twice_up = up + up
    new_down = jnp.minimum(
        jnp.maximum(down, jnp.minimum(twice_up, 0.0)), jnp.maximum(twice_up, 0.0)
    )
    new_up = jnp.minimum(
        jnp.maximum(up, jnp.minimum(twice_down, 0.0)), jnp.maximum(twice_down, 0.0)
    )
    return (center - new_down, center + new_up)


def euler_flux(state):
    density, mom_x, mom_y, mom_z, energy = state
    inverse = 1.0 / density
    velocity = mom_x * inverse
    carried = mom_x * velocity
    kinetic = 0.5 * (carried + (mom_y * mom_y + mom_z * mom_z) * inverse)
    pressure = (GAMMA - 1.0) * (energy - kinetic)
    fluxes = (
        mom_x,
        carried + pressure,
        mom_y * velocity,
        mom_z * velocity,
        (energy + pressure) * velocity,
    )
    signal = jnp.abs(velocity) + jnp.sqrt(GAMMA * pressure * inverse)
    return (fluxes, signal)


def double_flux(left, right):
    flux_left, signal_left = euler_flux(left)
    flux_right, signal_right = euler_flux(right)
    signal = jnp.maximum(signal_left, signal_right)
    return tuple(
        (fl + fr) - signal * (r - l) for fl, fr, l, r in zip(flux_left, flux_right, left, right)
    )


def lane_index(rows):
    return lax.broadcasted_iota(jnp.int32, (rows, LANES), 1)


def pull_lanes(value, index):
    return jnp.take_along_axis(value, index, axis=1)


def swept_cells(cell, first, last):
    values = {x: cell(x) for x in range(first - 3, last + 4)}
    edges = {}
    for x in range(first - 2, last + 2):
        edges[x] = [
            edge_value(*(values[x + o][f] for o in (-1, 0, 1, 2))) for f in range(FIELDS)
        ]
    limits = {}
    for x in range(first - 1, last + 2):
        limits[x] = [
            limit_edges(values[x][f], edges[x - 1][f], edges[x][f]) for f in range(FIELDS)
        ]
    flux = {}
    for x in range(first, last + 2):
        flux[x] = double_flux([p[1] for p in limits[x - 1]], [p[0] for p in limits[x]])
    return {
        x: [
            values[x][f] - 0.5 * STEP_RATIO * (flux[x + 1][f] - flux[x][f]) for f in range(FIELDS)
        ]
        for x in range(first, last + 1)
    }


def own_cell(own):
    def cell(x):
        return [
            own[pl.ds(f * CELLS + x, TILES, stride=FIELDS * CELLS), :] for f in range(FIELDS)
        ]

    return cell


def write_boxes(table, e, h, cells_of_age):
    lane = lane_index(TILES)
    upper_z = (lane & 8) != 0
    upper_y = (lane & 64) != 0

    def swap(low, high, upper, shift):
        return (
            jnp.where(upper, pltpu.roll(high, shift, 1), low),
            jnp.where(upper, high, pltpu.roll(low, LANES - shift, 1)),
        )

    for age, source in cells_of_age.items():
        for f in range(FIELDS):
            c0, c1, c2, c3 = [source[o][f] for o in range(4)]
            c0, c1 = swap(c0, c1, upper_z, 8)
            c2, c3 = swap(c2, c3, upper_z, 8)
            c0, c2 = swap(c0, c2, upper_y, 64)
            c1, c3 = swap(c1, c3, upper_y, 64)
            for q, value in enumerate((c0, c1, c2, c3)):
                row = (e * 8 + q * 2 + h) * GHOST_ROWS + age * FIELDS + f
                table[pl.ds(row, TILES, stride=16 * GHOST_ROWS), :] = value


def inner_kernel(own, table, kept):
    cell = own_cell(own)
    new = {}
    for first, last in ((3, 5), (8, 9), (14, 15), (18, 21), (24, 25)):
        new.update(swept_cells(cell, first, last))
    for i, x in enumerate(KEPT):
        for f in range(FIELDS):
            kept[6 + i, f] = new[x][f]
    for x in range(6):
        for f, value in enumerate(cell(x)):
            kept[x, f] = value
    for e, h, start in STARTS[1:]:
        where = [start + o for o in (-2, -1, 4, 5)]
        ages = {0: [cell(x) for x in where]}
        if e:
            ages[1] = [new[x] for x in where]
        write_boxes(table, e, h, ages)


def edge_kernel(codes, before, kept, table_in, sending, table, staged, sems):
    def cell(x):
        if x >= 0:
            return [kept[x, f] for f in range(FIELDS)]
        return [before[pl.ds(f * 8 + 8 + x, TILES, stride=FIELDS * 8), :] for f in range(FIELDS)]

    table[...] = table_in[...]
    new = swept_cells(cell, -2, -1)
    new.update(swept_cells(cell, 2, 2))
    for i, x in enumerate(KEPT):
        new[x] = [kept[6 + i, f] for f in range(FIELDS)]
    for e, h, start in STARTS[:2]:
        where = [start + o for o in (-2, -1, 4, 5)]
        ages = {1: [new[x] for x in where]}
        if h == 0:
            ages[0] = [cell(x) for x in where]
        write_boxes(table, e, h, ages)

    def send(k, carry):
        for c in range(2):
            base = (codes[2 * k + c] & (LANES - 1)) * GHOST_ROWS
            staged[k, 3 * c] = table[pl.ds(base, 4), :]
            staged[k, 3 * c + 1] = table[pl.ds(base + 4, 4), :]
            staged[k, 2, 2 * c : 2 * c + 2] = table[pl.ds(base + 8, 2), :]
        return carry

    chunks = sems.shape[0]
    size = staged.shape[0] // chunks
    copies = []
    for i in range(chunks):
        lax.fori_loop(i * size, (i + 1) * size, send, 0, unroll=8)
        part = slice(i * size, (i + 1) * size)
        copies.append(pltpu.make_async_copy(staged.at[part], sending.at[part], sems.at[i]))
        copies[-1].start()
    for copy in copies:
        copy.wait()


def coarse_kernel(
    codes, counts, live, own, before, after, final, fine_out, swept, face_out, lists, cells, fluxes
):
    size = FIELDS * FINE
    bound = live[0]

    def keep_live(s, carry):
        rows = pl.ds(pl.multiple_of(s * size, size), size)
        fine_out[rows, :] = jnp.where(s < bound, final[rows, :], 0.0)
        return carry

    lax.fori_loop(0, fine_out.shape[0] // size, keep_live, 0, unroll=2)
    stride = FIELDS * CELLS
    for f in range(FIELDS):
        for j in range(3):
            cells[j, f] = before[pl.ds(f * 8 + 5 + j, TILES, stride=FIELDS * 8), :]
            cells[35 + j, f] = after[pl.ds(f * 8 + j, TILES, stride=FIELDS * 8), :]

    def load_cells(x, carry):
        for f in range(FIELDS):
            cells[x + 3, f] = own[pl.ds(f * CELLS + x, TILES, stride=stride), :]
        return carry

    lax.fori_loop(0, CELLS, load_cells, 0, unroll=4)

    def limited(j, edge_before):
        edges, lefts, rights = ([], [], [])
        for f in range(FIELDS):
            edge = edge_value(cells[j - 1, f], cells[j, f], cells[j + 1, f], cells[j + 2, f])
            left, right = limit_edges(cells[j, f], edge_before[f], edge)
            edges.append(edge)
            lefts.append(left)
            rights.append(right)
        return (tuple(edges), tuple(lefts), tuple(rights))

    def advance(j, edges, rights):
        edges, lefts, next_rights = limited(j, edges)
        flux = double_flux(rights, lefts)
        for f in range(FIELDS):
            fluxes[j - 3, f] = flux[f]
        return (edges, next_rights, flux)

    edges = tuple(
        edge_value(cells[0, f], cells[1, f], cells[2, f], cells[3, f]) for f in range(FIELDS)
    )
    edges, _, rights = limited(2, edges)
    carry = advance(3, edges, rights)

    def step(x, carry):
        edges, rights, flux_before = carry
        edges, rights, flux = advance(x + 4, edges, rights)
        for f in range(FIELDS):
            swept[pl.ds(f * CELLS + x, TILES, stride=stride), :] = cells[
                x + 3, f
            ] - 0.5 * STEP_RATIO * (flux[f] - flux_before[f])
        return (edges, rights, flux)

    lax.fori_loop(0, CELLS, step, carry, unroll=4)
    for i, face in enumerate(FACES):
        for f in range(FIELDS):
            face_out[i, f] = 0.5 * fluxes[face, f]

    def collect(i, carry):
        total, first = carry
        code = codes[i] & (LANES - 1)
        entry = i * LANES + code
        lists[ALL_ITEMS + total] = entry
        lists[LEFT_ITEMS + first] = entry
        valid = lax.shift_right_logical(codes[i], 7) < counts[lax.shift_right_logical(i, 1)]
        leftmost = valid & ((code & 9) == 0)
        return (total + valid.astype(jnp.int32), first + leftmost.astype(jnp.int32))

    total, first = lax.fori_loop(0, codes.shape[0], collect, (0, 0), unroll=4)
    for i in range(MERGE_STEP):
        lists[ALL_ITEMS + total + i] = TILES * 16
        lists[LEFT_ITEMS + first + i] = TILES * 16
    lists[0] = lax.shift_right_logical(total + (MERGE_STEP - 1), 2)
    lists[1] = lax.shift_right_logical(first + (MERGE_STEP - 1), 2)


def fine_kernel(lookups, arrived, fine, after, final_out, back, ghosts, cells, packed, sems):
    slots = fine.shape[0] // (FIELDS * FINE)
    stride = FIELDS * FINE
    live = lookups[slots]

    def fetch(s, carry):
        look = lookups[s]
        owner = lax.shift_right_logical(look, 1)
        pos = look & 1
        ghosts[pl.ds(s, 4, stride=slots), :] = arrived[owner, 3 * pos]
        ghosts[pl.ds(s + 4 * slots, 4, stride=slots), :] = arrived[owner, 3 * pos + 1]
        ghosts[pl.ds(s + 8 * slots, 2, stride=slots), :] = arrived[owner, 2, pl.ds(2 * pos, 2)]
        return carry

    lax.fori_loop(0, slots, fetch, 0, unroll=8)

    lane = lane_index(BATCH)
    fine_y = lax.shift_right_logical(lane, 4)
    fine_z = lane & 15
    spread = lax.shift_right_logical(fine_y, 1) * 16 + lax.shift_right_logical(fine_z, 1)
    even_z = (lane & 1) == 0
    even_y = (lane & 16) == 0
    gather_back = (
        (2 * (fine_y & 3) + lax.shift_right_logical(lane, 6)) * 16
        + 2 * (lane & 7)
        + (lax.shift_right_logical(lane, 3) & 1)
    )

    def pair(first, second, even, shift):
        return jnp.where(even, first, pltpu.roll(second, shift, 1)) + jnp.where(
            even, pltpu.roll(first, LANES - shift, 1), second
        )

    def fold_four(scale, a, b, c, d):
        low = pair(a, b, even_z, 1)
        high = pair(c, d, even_z, 1)
        return pull_lanes(scale * pair(low, high, even_y, 16), gather_back)

    def put_ghosts(slot, rows):
        for f in range(FIELDS):
            first, second, third, fourth = [
                pull_lanes(rows[f], spread + (t // 2) * 64 + (t % 2) * 8) for t in range(4)
            ]
            cells[slot, 0, f] = first
            cells[slot, 1, f] = second
            cells[slot, 2, f] = second
            cells[slot, 11, f] = third
            cells[slot, 12, f] = third
            cells[slot, 13, f] = fourth

    def sweep(slot, keep):
        edges = None
        rights = None
        before = None
        bounds = []
        for j in range(1, 12):
            new_edges = [
                edge_value(
                    cells[slot, j - 1, f],
                    cells[slot, j, f],
                    cells[slot, j + 1, f],
                    cells[slot, j + 2, f],
                )
                for f in range(FIELDS)
            ]
            if edges is not None:
                pairs = [
                    limit_edges(cells[slot, j, f], edges[f], new_edges[f]) for f in range(FIELDS)
                ]
                if rights is not None:
                    flux = double_flux(rights, [p[0] for p in pairs])
                    if before is None:
                        bounds.append(flux)
                    else:
                        for f in range(FIELDS):
                            keep(
                                j - 4,
                                f,
                                cells[slot, j - 1, f]
                                - 0.5 * STEP_RATIO * (flux[f] - before[f]),
                            )
                    before = flux
                rights = [p[1] for p in pairs]
            edges = new_edges
        bounds.append(before)
        return bounds

    def put(s):
        source = pl.multiple_of(s * BACK_ROWS, BACK_ROWS)
        target = pl.multiple_of(lookups[s] * BACK_ROWS, BACK_ROWS)
        return pltpu.make_async_copy(
            packed.at[pl.ds(source, BACK_ROWS)], back.at[pl.ds(target, BACK_ROWS)], sems.at[s]
        )

    def group(g, carry):
        base = g * (BATCH * stride)
        rows = [
            ghosts[pl.ds(pl.multiple_of(r * slots + g * BATCH, 8), BATCH), :]
            for r in range(GHOST_ROWS)
        ]
        put_ghosts(0, rows[:FIELDS])
        put_ghosts(1, [0.5 * (o + n) for o, n in zip(rows[:FIELDS], rows[FIELDS:])])
        for x in range(FINE):
            for f in range(FIELDS):
                cells[0, x + 3, f] = fine[pl.ds(base + f * FINE + x, BATCH, stride=stride), :]

        def keep_middle(x, f, value):
            cells[1, x + 3, f] = value

        final = {}

        def keep_final(x, f, value):
            final[x, f] = value
            final_out[pl.ds(base + f * FINE + x, BATCH, stride=stride), :] = value

        first = sweep(0, keep_middle)
        second = sweep(1, keep_final)
        rows = []
        for f in range(FIELDS):
            rows.append(
                fold_four(0.125, *[final[2 * t, f] + final[2 * t + 1, f] for t in range(4)])
            )
        faces = [first[side][f] + second[side][f] for side in range(2) for f in range(FIELDS)]
        faces += [faces[-1], faces[-1]]
        for t in range(3):
            rows.append(fold_four(0.0625, *faces[4 * t : 4 * t + 4]))
        for r, value in enumerate(rows):
            packed[pl.ds(g * (BATCH * BACK_ROWS) + r, BATCH, stride=BACK_ROWS), :] = value
        for i in range(BATCH):
            s = g * BATCH + i

            @pl.when(s < live)
            def _():
                put(s).start()

        return carry

    lax.fori_loop(0, slots // BATCH, group, 0)

    def finish(s, carry):
        @pl.when(s < live)
        def _():
            put(s).wait()

        return carry

    lax.fori_loop(0, slots, finish, 0, unroll=8)


def quad_offset(code):
    quad = lax.shift_right_logical(code, 1) & 3
    return lax.shift_right_logical(quad, 1) * 64 + (quad & 1) * 8


def to_quad(value, offset, t):
    return pltpu.roll(value, (offset + LANES - ((t // 2) * 64 + (t % 2) * 8)) & (LANES - 1), 1)


def came_item(came, entry):
    row = lax.shift_right_logical(entry, 7) * BACK_ROWS
    return came[pl.ds(pl.multiple_of(row, BACK_ROWS), BACK_ROWS), :]


def left_kernel(lists, came, face_in, left_out):
    for f in range(FIELDS):
        left_out[f] = jnp.zeros((TILES, LANES), jnp.float32)
    quads = lane_index(1) & 72

    def scatter(n, carry):
        for i in range(MERGE_STEP):
            entry = lists[LEFT_ITEMS + n * MERGE_STEP + i]
            code = entry & (LANES - 1)
            offset = quad_offset(code)
            tile = pl.ds(jnp.minimum(lax.shift_right_logical(code, 4), TILES - 1), 1)
            value = came_item(came, entry)
            moved = [to_quad(value, offset, t) for t in range(4)]
            inside = quads == jnp.where(code < TILES * 16, offset, LANES)
            for f in range(FIELDS):
                row = FIELDS + f // 4
                fix = STEP_RATIO * (face_in[0, f, tile] - moved[f % 4][row : row + 1])
                pltpu.store(left_out.at[f, tile], fix, mask=inside)
        return carry

    lax.fori_loop(0, lists[1], scatter, 0)


def merge_kernel(lists, came, swept, face_in, left_in, out, field, cover):
    out[...] = swept[...]
    stride = FIELDS * CELLS
    for i in range(TILES * 2):
        cover[8 * i : 8 * i + 8, :] = jnp.zeros((8, LANES), jnp.float32)
    quads = lane_index(8) & 72

    ones = jnp.ones((4, LANES), jnp.float32)

    def scatter(n, carry):
        for i in range(MERGE_STEP):
            entry = lists[ALL_ITEMS + n * MERGE_STEP + i]
            code = entry & (LANES - 1)
            offset = quad_offset(code)
            line = lax.shift_right_logical(code, 3) * 8 + (code & 1) * 4
            value = came_item(came, entry)
            inside = quads == offset
            for t in range(4):
                rows = pl.ds(pl.multiple_of((line + t) * 8, 8), 8)
                pltpu.store(field.at[rows, :], to_quad(value, offset, t), mask=inside)
            pltpu.store(cover.at[pl.ds(line, 4), :], ones, mask=inside[:4])
        return carry

    lax.fori_loop(0, lists[0], scatter, 0)

    for t in range(TILES):
        for e in range(2):
            hit = cover[pl.ds(t * 16 + e * 8, 8), :] > 0.5
            for f in range(FIELDS):
                row = t * stride + f * CELLS + e * 16
                value = field[pl.ds((t * 16 + e * 8) * 8 + f, 8, stride=8), :]
                pltpu.store(out.at[row : row + 8, :], value, mask=hit)

    for e, h, start in STARTS:
        line = e * 8 + h * 4
        hit = cover[pl.ds(line, TILES, stride=16), :] > 0.5
        for side in range(2):
            cell = start + 4 if side else start - 1
            if cell < 0:
                continue
            for f in range(FIELDS):
                item = side * FIELDS + f
                face = field[
                    pl.ds((line + item % 4) * 8 + FIELDS + item // 4, TILES, stride=128), :
                ]
                coarse = face_in[FACES.index(start + 4 * side), f]
                fix = STEP_RATIO * ((face - coarse) if side else (coarse - face))
                fix = jnp.where(hit, fix, 0.0)
                rows = pl.ds(f * CELLS + cell, TILES, stride=stride)
                out[rows, :] = out[rows, :] + fix


def last_kernel(incoming, merged, out):
    out[...] = merged[...]
    for f in range(FIELDS):
        for t in range(TILES):
            cell = slice(CELLS - 1, CELLS)
            out[t, f, cell, :] = merged[t, f, cell, :] + incoming[f, t : t + 1, :]


def in_vmem():
    return pl.BlockSpec(memory_space=pltpu.VMEM)


def in_smem():
    return pl.BlockSpec(memory_space=pltpu.SMEM)


def anywhere():
    return pl.BlockSpec(memory_space=pl.ANY)


def shaped(*dims):
    return jax.ShapeDtypeStruct(dims, jnp.float32)


def body(coarse_state, fine_state, fine_count, parent_owner, parent_site, fine_half):
    groups = lax.axis_size("gy")
    rows_x = lax.axis_size("gx")
    me = lax.axis_index("gy")
    slots = fine_state.shape[1]
    params = pltpu.CompilerParams(vmem_limit_bytes=VMEM)

    up = [(i, (i + 1) % rows_x) for i in range(rows_x)]
    down = [(j, i) for i, j in up]
    before = lax.ppermute(coarse_state[:, :, CELLS - 8 :], "gx", up)
    after = lax.ppermute(coarse_state[:, :, :8], "gx", down)
    whole, before, after = (v.reshape(-1, LANES) for v in (coarse_state, before, after))

    order = jnp.arange(slots, dtype=jnp.int32)
    joined = parent_owner * LANES + parent_site * 2 + fine_half
    joined = joined.reshape(groups, slots)
    hit = lax.shift_right_logical(joined, 7) == me
    key = order[None, :] * LANES + (joined & (LANES - 1))
    key = jnp.where(hit, key, slots * LANES)
    low = jnp.min(key, axis=1)
    next_low = jnp.min(jnp.where(key > low[:, None], key, slots * LANES), axis=1)
    codes = jnp.stack([low, next_low], axis=1).reshape(2 * groups)
    counts = fine_count.reshape(groups)
    mine = lax.dynamic_index_in_dim(joined, me, 0, keepdims=False)
    mine = lax.shift_right_logical(mine, 7)
    live = lax.dynamic_slice_in_dim(counts, me, 1, 0)
    twin = (mine[:, None] == mine[None, :]) & (order[None, :] < order[:, None])
    lookups = jnp.concatenate([2 * mine + jnp.any(twin, axis=1).astype(jnp.int32), live])

    table_shape = shaped(TILES * 16 * GHOST_ROWS, LANES)
    table, kept = pl.pallas_call(
        inner_kernel,
        out_shape=(table_shape, shaped(6 + len(KEPT), FIELDS, TILES, LANES)),
        in_specs=[in_vmem()],
        out_specs=(in_vmem(), in_vmem()),
        cost_estimate=pl.CostEstimate(flops=4_000_000, bytes_accessed=3_000_000, transcendentals=0),
        compiler_params=params,
        name="inner",
    )(whole)
    sending = pl.pallas_call(
        edge_kernel,
        out_shape=shaped(groups, 5, 4, LANES),
        in_specs=[in_smem(), in_vmem(), in_vmem(), in_vmem()],
        out_specs=anywhere(),
        scratch_shapes=[
            pltpu.VMEM(table_shape.shape, jnp.float32),
            pltpu.VMEM((groups, 5, 4, LANES), jnp.float32),
            pltpu.SemaphoreType.DMA((4,)),
        ],
        compiler_params=params,
        name="edge",
    )(codes, before, kept, table)
    arrived = lax.all_to_all(sending, "gy", split_axis=0, concat_axis=0, tiled=True)

    final, back = pl.pallas_call(
        fine_kernel,
        out_shape=(
            shaped(slots * FIELDS * FINE, LANES),
            shaped(groups * 2 * BACK_ROWS, LANES),
        ),
        in_specs=[in_smem(), in_vmem(), in_vmem(), in_vmem()],
        out_specs=(in_vmem(), anywhere()),
        scratch_shapes=[
            pltpu.VMEM((GHOST_ROWS * slots, LANES), jnp.float32),
            pltpu.VMEM((2, FINE + 6, FIELDS, BATCH, LANES), jnp.float32),
            pltpu.VMEM((slots * BACK_ROWS, LANES), jnp.float32),
            pltpu.SemaphoreType.DMA((slots,)),
        ],
        compiler_params=params,
        name="fine",
    )(lookups, arrived, fine_state.reshape(-1, LANES), after)
    fine_out, swept, faces, lists = pl.pallas_call(
        coarse_kernel,
        out_shape=(
            shaped(slots * FIELDS * FINE, LANES),
            shaped(TILES * FIELDS * CELLS, LANES),
            shaped(len(FACES), FIELDS, TILES, LANES),
            jax.ShapeDtypeStruct((512,), jnp.int32),
        ),
        in_specs=[in_smem(), in_smem(), in_smem()] + [in_vmem()] * 4,
        out_specs=(in_vmem(), in_vmem(), in_vmem(), in_smem()),
        scratch_shapes=[
            pltpu.VMEM((CELLS + 6, FIELDS, TILES, LANES), jnp.float32),
            pltpu.VMEM((CELLS + 1, FIELDS, TILES, LANES), jnp.float32),
        ],
        cost_estimate=pl.CostEstimate(
            flops=10_000_000, bytes_accessed=12_000_000, transcendentals=0
        ),
        compiler_params=params,
        name="coarse",
    )(codes, counts, live, whole, before, after, final)
    came = lax.all_to_all(
        back.reshape(groups, 2 * BACK_ROWS, LANES), "gy", split_axis=0, concat_axis=0, tiled=True
    )

    came = came.reshape(-1, LANES)
    left_fix = pl.pallas_call(
        left_kernel,
        out_shape=shaped(FIELDS, TILES, LANES),
        in_specs=[in_smem(), in_vmem(), in_vmem()],
        out_specs=in_vmem(),
        compiler_params=params,
        name="left",
    )(lists, came, faces)
    incoming = lax.ppermute(left_fix, "gx", down)
    merged = pl.pallas_call(
        merge_kernel,
        out_shape=shaped(TILES * FIELDS * CELLS, LANES),
        in_specs=[
            in_smem(),
            in_vmem(),
            in_vmem(),
            in_vmem(),
            anywhere(),
        ],
        out_specs=in_vmem(),
        scratch_shapes=[
            pltpu.VMEM(((TILES * 16 + 8) * 8, LANES), jnp.float32),
            pltpu.VMEM((TILES * 16 + 8, LANES), jnp.float32),
        ],
        cost_estimate=pl.CostEstimate(flops=2_000_000, bytes_accessed=8_000_000, transcendentals=0),
        compiler_params=params,
        name="merge",
    )(lists, came, swept, faces, left_fix)
    coarse_out = pl.pallas_call(
        last_kernel,
        out_shape=shaped(TILES, FIELDS, CELLS, LANES),
        in_specs=[in_vmem(), in_vmem()],
        out_specs=in_vmem(),
        compiler_params=params,
        name="last",
    )(incoming, merged.reshape(TILES, FIELDS, CELLS, LANES))
    return (coarse_out, fine_out.reshape(fine_state.shape))


def solution(mesh):
    placed = (
        P("gy", None, "gx", None),
        P("gx", "gy", None, None, None),
        P("gx", None),
        P("gx", None),
        P("gx", None),
        P("gx", None),
    )
    return jax.shard_map(
        body,
        mesh=mesh,
        in_specs=placed,
        out_specs=(P("gy", None, "gx", None), P("gx", "gy", None, None, None)),
        check_vma=False,
    )
```
